256 devices in a mesh: dp: 16 (over z_hi, y), expert: 16 (over z_lo, x, core).
Axes of the slice: x: 4, y: 4, z: 8 (z_hi: 4, z_lo: 2; z = z_hi * 2 + z_lo), core: 2. Of those that a mesh axis runs over, the one named last changes fastest.
Arguments:
- out_grad: bfloat16 [32768, 5120], P(('dp', 'expert')), may hold values from -6 to 6
- router_logits: float32 [32768, 16], P(('dp', 'expert')), may hold values from -5 to 303
- choice_ids: int32 [32768, 6], P(('dp', 'expert')), may hold values from 0 to 15, all different within a row; in each aligned block of 128 rows (0 to 127, 128 to 255, ...) at most 56 rows name the same one
- hidden: bfloat16 [16, 16, 16, 56, 768], P('dp', 'expert'), may hold values from -0.625 to 0.625
- master: float32 [768, 16, 5120], P('dp', 'expert'), may hold values from -0.21875 to 0.21875
- first: float32 [768, 16, 5120], P('dp', 'expert'), may hold values from -6 to 6
- second: float32 [768, 16, 5120], P('dp', 'expert'), may hold values from 0.1 to 10
Outputs:
- new_weight: float32 [768, 16, 5120], P('dp', 'expert')
- new_first: float32 [768, 16, 5120], P('dp', 'expert')
- new_second: float32 [768, 16, 5120], P('dp', 'expert')
- router_grad: float32 [32768, 16], P(('dp', 'expert'))
The draws below stay inside these ranges and needn't reach their ends.
Inputs may be any that keep to these rules, and one draw needn't show every extreme that they name: `choice_ids`: each row names 6 different experts. In the rows of one device no expert is named more than 56 times, and in some device's rows some expert is named exactly 56 times.
All inputs are finite; a program needn't handle non-finite values.
Results may differ from the reference program's by a relative error of at most 0.0035.
Values may be sent and summed in bfloat16 or wider, within the bound.
A program may use at most 128 MiB of HBM per device.

```python
import math
import jax
import jax.numpy as jnp
import numpy as np
from jax import lax

D = 5120
FF = 768
EXPERTS = 16
TOPK = 6
T_DEV = 128
CAP = 56
TOKENS = 32768
N_DP = 16
N_EXPERT = 16


def draw_router_logits(key, part):
    key = jax.random.fold_in(key, 11)
    keys = jax.random.split(key, 1)
    base = jax.random.normal(keys[0], (TOKENS, EXPERTS), jnp.float32) * 1.5
    return jnp.clip(base, -5.0, 5.0)


def strengthened(drawn, stream_key, source, target, shards_of, factor):
    owner, partner = [(jnp.arange(drawn.shape[position]) // (drawn.shape[position] // shards_of)).reshape([-1 if axis == position else 1 for axis in range(drawn.ndim)]) for position in (source, target)]
    chosen = jax.random.permutation(stream_key, shards_of)[partner]
    strong = (owner == chosen) | (owner == (partner + shards_of // 2) % shards_of)
    return jnp.where(strong, factor * drawn, drawn)


def levels(own_key, dims, pieces, low, largest):
    def one(position, blocks):
        draws = jax.random.uniform(jax.random.fold_in(jax.random.fold_in(own_key, 6), position), (blocks,), jnp.float32, low / len(pieces), largest / len(pieces))
        return jnp.repeat(jnp.exp(draws), dims[position] // blocks).reshape((-1,) + (1,) * (len(dims) - position - 1))

    level = one(*pieces[0])
    for cut in pieces[1:]:
        level = level * one(*cut)
    return level


def deal_out(key, own, number, rows, amount, top, bound, skew):
    ranking = jax.random.permutation(key, amount)
    packed, common = shares(amount, rows * top, bound, skew, True), shares(amount, rows * top, bound, skew, False)
    places = jnp.arange(amount)

    def named(sizes, turn):
        used = int((sizes > 0).sum())
        fixed = max(1, used // 4)
        passed = fixed + (places - fixed + turn * (used - fixed)) % max(1, amount - fixed)
        return jnp.zeros((amount,), jnp.int32).at[ranking[jnp.where(places < fixed, places, passed)]].set(jnp.asarray(sizes, jnp.int32))

    sizes = jnp.where(number % 4 == 0, named(packed, number // 4), named(common, number - number // 4 - 1))
    mixed = jax.random.permutation(jax.random.fold_in(own, 3), amount)
    source_of, receiver = mixed[0:amount // 2 * 2:2], mixed[1:amount // 2 * 2:2]
    slack = jnp.minimum(sizes[source_of] - 1, bound - sizes[receiver]) // 2
    slack = jnp.where((source_of == ranking[0]) | (receiver == ranking[0]) | (sizes[receiver] == 0), 0, jnp.maximum(slack, 0))
    passed = jax.random.randint(jax.random.fold_in(own, 4), (amount // 2,), 0, 1 << 20) % (slack + 1)
    sizes = sizes.at[source_of].add(-passed).at[receiver].add(passed)
    items = jnp.searchsorted(jnp.cumsum(sizes), jnp.arange(rows * top), side="right").astype(jnp.int32)
    listing = items.reshape(top, rows).T
    listing = listing[jax.random.permutation(jax.random.fold_in(own, 1), rows)]
    turn = jax.random.randint(jax.random.fold_in(own, 2), (rows, 1), 0, top)
    return jnp.take_along_axis(listing, (jnp.arange(top)[None, :] + turn) % top, axis=1)


def shares(number_of, total, limit, lean, full):
    portions = [(1 << 20) // math.isqrt(grade ** lean) + 1 for grade in range(1, number_of + 1)]
    largest = limit if full else min(limit, max(-(-total // number_of), total * portions[0] // sum(portions)))
    least = 1 if total - largest >= number_of - 1 else 0
    given, surplus = [largest] + [least] * (number_of - 1), total - largest - least * (number_of - 1)
    while surplus > 0:
        candidates = [i for i in range(1, number_of) if given[i] < largest] or [i for i in range(1, number_of) if given[i] < limit]
        mass, remaining = sum([portions[i] for i in candidates]), surplus
        for i in candidates:
            more = min(limit - given[i], max(1, remaining * portions[i] // mass), surplus)
            given[i] = given[i] + more
            surplus = surplus - more
    return np.array(given)


def centred(own_key, extent, width, most, cuts=(), held_as=jnp.bfloat16):
    array = jax.random.normal(own_key, extent, jnp.float32) * width
    if len(cuts) > 0:
        array = levels(own_key, extent, cuts, -0.22, 0.18) * array
    return jnp.clip(array, min=-most, max=most).astype(held_as)


def gaussian_with(key, extent, scale, most, shards, heavy, kind=jnp.bfloat16):
    array = scale * jax.random.normal(key, extent, jnp.float32)
    if shards:
        array = array * levels(key, extent, shards, -0.22, 0.18)
    return jnp.clip(strengthened(array, jax.random.fold_in(key, 3), *heavy), -most, most).astype(kind)


def setup_inputs(seed: int = 0) -> dict:
    streams_of = jax.random.split(jax.random.key(seed), 8)
    out_grad = centred(streams_of[0], (TOKENS, D), 1.0, 6.0, ((0, 256),))
    router_logits = draw_router_logits(jax.random.fold_in(streams_of[7], 71), 0)
    choice_ids_keys = jax.random.split(jax.random.fold_in(streams_of[2], 1), TOKENS // T_DEV)
    choice_ids_turns = jax.random.permutation(jax.random.fold_in(streams_of[2], 3), TOKENS // T_DEV)
    choice_ids = jax.vmap(lambda own, number: deal_out(jax.random.fold_in(streams_of[2], 2), own, number, T_DEV, EXPERTS, TOPK, CAP, 2))(choice_ids_keys, choice_ids_turns).reshape((TOKENS, TOPK))
    hidden = gaussian_with(streams_of[3], (N_DP, EXPERTS, N_EXPERT, CAP, FF), 0.08, 0.625, ((0, 16), (1, 16)), (0, 4, 16, 2.0))
    master = centred(streams_of[4], (FF, EXPERTS, D), FF ** -0.5, 0.21875, ((0, 16), (1, 16)), jnp.float32)
    first = centred(streams_of[5], (FF, EXPERTS, D), 1.0, 6.0, ((0, 16), (1, 16)), jnp.float32)
    second = jnp.clip(jnp.exp(math.log(10.0) - 4.6051702 * jax.random.uniform(streams_of[6], (FF, EXPERTS, D), jnp.float32) ** levels(streams_of[6], (FF, EXPERTS, D), ((0, 16), (1, 16)), -0.2, 0.2)), 0.1, 10.0)
    return {"out_grad": out_grad, "router_logits": router_logits, "choice_ids": choice_ids, "hidden": hidden, "master": master, "first": first, "second": second}


beta_one = 0.9
beta_two = 0.95
learn_rate = 0.001
decay_rate = 0.1
epsilon = 1e-08
adam_step = 100.0

def pair_slots(choice_block, experts, capacity):
    tokens_here, picks = choice_block.shape
    flat_ids = choice_block.reshape(-1)
    labels = jnp.arange(experts, dtype=jnp.int32)
    onehot = (flat_ids[:, None] == labels[None, :]).astype(jnp.int32)
    earlier = jnp.cumsum(onehot, axis=0) - onehot
    slot_of = lax.optimization_barrier(jnp.sum(earlier * onehot, axis=1)).astype(jnp.int32)
    pair_index = jnp.arange(tokens_here * picks, dtype=jnp.int32)
    table = jnp.full((experts * capacity,), tokens_here * picks, jnp.int32)
    table = table.at[flat_ids * capacity + slot_of].set(pair_index)
    return (flat_ids, slot_of, table)

def dispatch_block(rows_block, choice_block, prob_block):
    flat_ids, slot_of, table = pair_slots(choice_block, EXPERTS, CAP)
    pair_prob = jnp.take_along_axis(prob_block, choice_block, axis=1).reshape(-1).astype(jnp.bfloat16)
    sent = jnp.take(rows_block, table // TOPK, axis=0, mode='fill', fill_value=0).reshape(EXPERTS, CAP, D)
    sent_prob = jnp.take(pair_prob, table, axis=0, mode='fill', fill_value=0).reshape(EXPERTS, CAP)
    return (sent, sent_prob)

def route_grad(choice_block, prob_block, back_scores):
    flat_ids, slot_of, table = pair_slots(choice_block, EXPERTS, CAP)
    pair_score = back_scores.reshape(-1)[flat_ids * CAP + slot_of].reshape(T_DEV, TOPK)
    labels = jnp.arange(EXPERTS, dtype=jnp.int32)
    onehot = choice_block[:, :, None] == labels[None, None, :]
    gain = lax.optimization_barrier(jnp.sum(jnp.where(onehot, pair_score[:, :, None], 0.0), axis=1))
    return prob_block * (gain - lax.optimization_barrier(jnp.sum(prob_block * gain, axis=1, keepdims=True)))

def reference(out_grad, router_logits, choice_ids, hidden, master, first, second):
    probs = jax.nn.softmax(router_logits, axis=-1)
    blocks_rows = out_grad.reshape(N_DP, N_EXPERT, T_DEV, D)
    blocks_ids = choice_ids.reshape(N_DP, N_EXPERT, T_DEV, TOPK)
    blocks_prob = probs.reshape(N_DP, N_EXPERT, T_DEV, EXPERTS)
    weight_by_expert = jnp.swapaxes(master.astype(jnp.bfloat16), 0, 1)

    def one_expert(inputs):
        rows_e, prob_e, saved_e, weight_e = inputs
        rows_flat = rows_e.reshape(N_EXPERT * CAP, D)
        saved_flat = saved_e.reshape(N_EXPERT * CAP, FF)
        back = jnp.dot(rows_flat, weight_e.T, preferred_element_type=jnp.float32)
        score = lax.optimization_barrier(jnp.sum(saved_flat.astype(jnp.float32) * back, axis=1))
        scaled = (prob_e.reshape(-1, 1).astype(jnp.float32) * rows_flat.astype(jnp.float32)).astype(jnp.bfloat16)
        partial_sum = jnp.dot(saved_flat.T, scaled, preferred_element_type=jnp.float32).astype(jnp.bfloat16)
        return (score.reshape(N_EXPERT, CAP), partial_sum)

    def one_row(total, inputs):
        rows_d, ids_d, prob_d, saved_d = inputs
        sent, sent_prob = jax.vmap(dispatch_block)(rows_d, ids_d, prob_d)
        scores, partials = lax.map(one_expert, (jnp.swapaxes(sent, 0, 1), jnp.swapaxes(sent_prob, 0, 1), saved_d, weight_by_expert))
        total = total + jnp.swapaxes(partials, 0, 1).astype(jnp.float32)
        return (total, scores)
    zeros = jnp.zeros((FF, EXPERTS, D), jnp.float32)
    grad, scores_all = lax.scan(one_row, zeros, (blocks_rows, blocks_ids, blocks_prob, hidden))
    returned = jnp.transpose(scores_all, (0, 2, 1, 3))
    router_grad = jax.vmap(jax.vmap(route_grad))(blocks_ids, blocks_prob, returned).reshape(TOKENS, EXPERTS)
    new_first = beta_one * first + (1.0 - beta_one) * grad
    new_second = beta_two * second + (1.0 - beta_two) * grad * grad
    first_hat = new_first / (1.0 - beta_one ** adam_step)
    second_hat = new_second / (1.0 - beta_two ** adam_step)
    new_weight = master - learn_rate * (first_hat / (jnp.sqrt(second_hat) + epsilon) + decay_rate * master)
    return (new_weight, new_first, new_second, router_grad)
```

```python
import functools

import jax
import jax.numpy as jnp
from jax import lax
from jax.experimental import pallas as pl
from jax.experimental.pallas import tpu as pltpu
from jax.sharding import PartitionSpec as P

beta_one = 0.9
beta_two = 0.95
learn_rate = 0.001
decay_rate = 0.1
epsilon = 1e-08
adam_step = 100.0

MESH = pl.DeviceIdType.MESH
F32 = jnp.float32
BF16 = jnp.bfloat16

NZ, NY, NX = 4, 4, 4
PARTS = 10
KEEP = 4

Z_OWN, XP_OWN, XM_OWN, SIB_OWN = 0, 1, 2, 3
XP_PART, XM_PART, SIB_PART = 4, 5, 6
XP_FWD, XM_FWD = 7, 8
SIB_X = 9
SIB_F = 13
WZP, WZM, WZF, WYP, WYM, WYPF, WYMF = 15, 16, 17, 18, 19, 20, 21
FYP, FYM, RYP, RYM, FZP, FZM, RZP, RZM = 22, 23, 24, 25, 26, 27, 28, 29
KINDS = 30

LAG_C = 4


def kernel(
    og, ids, logits, hid, wl, grad_out, router_out,
    G, W, PB, FP, FM, RP, RM, S, ZFP, ZFM, ZRP, ZRM,
    HT, OH, ROWS, SCALED, ACC, CS, CR, GS, GR, PT,
    ss, rs, l1, l2, cs_s, cs_r, gs_s, gs_r,
):
    nc, experts, t_dev, C = G.shape
    rows_all, ff = hid.shape
    cap = rows_all // experts
    half = C // 2
    d = lax.axis_index("dp")
    e = lax.axis_index("expert")
    z, y = d // NY, d % NY
    zl, x, core = e // (2 * NX), (e // 2) % NX, e % 2
    up = lambda v: (v + 1) % 4
    down = lambda v: (v + 3) % 4
    opp = lambda v: (v + 2) % 4
    eid = lambda a, b, c: a * (2 * NX) + b * 2 + c
    did = lambda a, b: a * NY + b

    part = (d, eid(1 - zl, x, core))
    xp = (d, eid(zl, up(x), core))
    xm = (d, eid(zl, down(x), core))
    sib = (d, eid(zl, x, 1 - core))
    zp = (did(up(z), y), e)
    zm = (did(down(z), y), e)
    yp = (did(z, up(y)), e)
    ym = (did(z, down(y)), e)

    def rc(kind, j, src, dst, dev):
        return pltpu.make_async_remote_copy(
            src_ref=src, dst_ref=dst, send_sem=ss.at[kind, j], recv_sem=rs.at[kind, j],
            device_id=dev, device_id_type=MESH,
        )

    def cols(j, width=C):
        return pl.ds(pl.multiple_of(j * C, C), width)

    def local_g(j):
        return pltpu.make_async_copy(og.at[:, cols(j)], G.at[j, e], l1.at[j])

    def local_w(j):
        return pltpu.make_async_copy(wl.at[:, cols(j)], W.at[j, z, y], l2.at[j])

    def stage_local(j, carry):
        local_g(j).start()
        local_w(j).start()
        return carry

    lax.fori_loop(0, nc, stage_local, 0)

    barrier = pltpu.get_barrier_semaphore()

    def greet(k, carry):
        pl.semaphore_signal(barrier, inc=1, device_id=(d, (e + k) % experts), device_id_type=MESH)
        return carry

    lax.fori_loop(1, experts, greet, 0)
    for dev in (zp, zm, yp, ym):
        pl.semaphore_signal(barrier, inc=1, device_id=dev, device_id_type=MESH)
    pl.semaphore_wait(barrier, experts - 1 + 4)

    def block(j, a, b, c):
        return G.at[j, eid(a, b, c)]

    def d_send(kind, j, a, b, dev):
        ref = block(j, a, b, core)
        return rc(kind, j, ref, ref, dev)

    def d_recv(kind, j, a, b, c):
        ref = block(j, a, b, c)
        return rc(kind, j, ref, ref, sib)

    def w_copy(kind, j, ref, dev):
        return rc(kind, j, ref, ref, dev)

    def pslot(j):
        return j % KEEP

    def c_copy(peer, source):
        return pltpu.make_async_remote_copy(
            src_ref=CS.at[peer], dst_ref=CR.at[source], send_sem=cs_s.at[peer], recv_sem=cs_r.at[source],
            device_id=(d, peer), device_id_type=MESH,
        )

    def g_copy(peer, source):
        return pltpu.make_async_remote_copy(
            src_ref=GS.at[peer], dst_ref=GR.at[source], send_sem=gs_s.at[peer], recv_sem=gs_r.at[source],
            device_id=(d, peer), device_id_type=MESH,
        )

    def at_stage(i, lag, fn):
        j = i - lag

        @pl.when(jnp.logical_and(j >= 0, j < nc))
        def _():
            fn(j)

    def stage0(j):
        local_g(j).wait()
        local_w(j).wait()
        d_send(Z_OWN, j, zl, x, part).start()
        d_send(XP_OWN, j, zl, x, xp).start()
        d_send(XM_OWN, j, zl, x, xm).start()
        d_send(SIB_OWN, j, zl, x, sib).start()
        w_copy(WZP, j, W.at[j, z, y], zp).start()
        w_copy(WZM, j, W.at[j, z, y], zm).start()

    def stage1(j):
        d_recv(Z_OWN, j, 1 - zl, x, core).wait_recv()
        d_send(XP_PART, j, 1 - zl, x, xp).start()
        d_send(XM_PART, j, 1 - zl, x, xm).start()
        d_send(SIB_PART, j, 1 - zl, x, sib).start()
        w_copy(WZP, j, W.at[j, down(z), y], zp).wait_recv()
        w_copy(WZM, j, W.at[j, up(z), y], zm).wait_recv()

        @pl.when(j % 2 == 0)
        def _():
            w_copy(WZF, j, W.at[j, down(z), y], zp).start()

        @pl.when(j % 2 == 1)
        def _():
            w_copy(WZF, j, W.at[j, up(z), y], zm).start()

    def stage2(j):
        d_recv(XP_OWN, j, zl, down(x), core).wait_recv()
        d_recv(XM_OWN, j, zl, up(x), core).wait_recv()
        d_recv(XP_PART, j, 1 - zl, down(x), core).wait_recv()
        d_recv(XM_PART, j, 1 - zl, up(x), core).wait_recv()
        d_send(XP_FWD, j, 0, down(x), xp).start()
        d_send(XM_FWD, j, 1, up(x), xm).start()
        w_copy(WZF, j, W.at[j, opp(z), y], zp).wait_recv()
        w_copy(WYP, j, W.at[j, :, y], yp).start()
        w_copy(WYM, j, W.at[j, :, y], ym).start()
        for k, (a, b) in enumerate(((0, down(x)), (1, down(x)), (0, up(x)), (1, up(x)))):
            d_send(SIB_X + k, j, a, b, sib).start()

    def stage3(j):
        w_copy(WYP, j, W.at[j, :, down(y)], yp).wait_recv()
        w_copy(WYM, j, W.at[j, :, up(y)], ym).wait_recv()
        w_copy(WYPF, j, W.at[j, 0:2, down(y)], yp).start()
        w_copy(WYMF, j, W.at[j, 2:4, up(y)], ym).start()
        d_recv(XP_FWD, j, 0, opp(x), core).wait_recv()
        d_recv(XM_FWD, j, 1, opp(x), core).wait_recv()
        for k in range(2):
            d_send(SIB_F + k, j, k, opp(x), sib).start()

    def setup_select():
        def wait_code(k, carry):
            c_copy((e + k) % experts, (e + k) % experts).wait_recv()
            return carry

        lax.fori_loop(1, experts, wait_code, 0)
        CR[pl.ds(e, 1)] = CS[pl.ds(e, 1)]
        slots = lax.broadcasted_iota(jnp.int32, (cap, t_dev), 0).astype(F32)
        empty = jnp.zeros((cap, t_dev), F32)
        for p in range(experts // 2):
            one, weighted = [], []
            for s in range(2):
                tile = CR[2 * p + s]
                hot = jnp.where(slots == tile[0:1, :], 1.0, 0.0)
                gate = hot * tile[1:2, :]
                one.append(jnp.concatenate([hot, empty] if s == 0 else [empty, hot], axis=1))
                weighted.append(jnp.concatenate([gate, empty] if s == 0 else [empty, gate], axis=1))
            OH[p] = jnp.concatenate(one + weighted, axis=0).astype(BF16)

    def stage_c(j):
        @pl.when(j == 0)
        def _():
            setup_select()

        other = 1 - core
        d_recv(SIB_OWN, j, zl, x, other).wait_recv()
        d_recv(SIB_PART, j, 1 - zl, x, other).wait_recv()
        for k, (a, b) in enumerate(((0, down(x)), (1, down(x)), (0, up(x)), (1, up(x)))):
            d_recv(SIB_X + k, j, a, b, other).wait_recv()
        for k in range(2):
            d_recv(SIB_F + k, j, k, opp(x), other).wait_recv()

        pair = 2 * cap
        for p in range(experts // 2):
            tokens = G[j, 2 * p : 2 * p + 2].reshape(2 * t_dev, C)
            picked = jnp.dot(OH[p], tokens, preferred_element_type=F32)
            ROWS[p * pair : (p + 1) * pair, :] = picked[:pair].astype(BF16)
            SCALED[p * pair : (p + 1) * pair, :] = picked[pair:].astype(BF16)

        slot = pslot(j)

        @pl.when(j >= KEEP)
        def _():
            release(j - KEEP)

        partial = jnp.dot(HT[...], SCALED[...], preferred_element_type=F32)
        PB[slot] = partial.astype(BF16).reshape(NZ, NY, ff // (NZ * NY), C)
        rc(FYP, j, PB.at[slot, 2:4, opp(y)], FP.at[j], yp).start()
        rc(FYM, j, PB.at[slot, 0:2, opp(y)], FM.at[j], ym).start()

        w_copy(WYPF, j, W.at[j, 0:2, opp(y)], yp).wait_recv()
        w_copy(WYMF, j, W.at[j, 2:4, opp(y)], ym).wait_recv()
        through = jnp.dot(hid[...], W[j].reshape(ff, C), preferred_element_type=F32)
        product = through * ROWS[...].astype(F32)
        total = product[:, 0:128]
        for k in range(1, C // 128):
            total = total + product[:, k * 128 : (k + 1) * 128]
        ACC[...] += total

        @pl.when(j == nc - 1)
        def _():
            send_scores()

    def send_scores():
        score = jnp.sum(ACC[...], axis=1, keepdims=True)
        slots = lax.broadcasted_iota(jnp.int32, (cap, t_dev), 0).astype(F32)
        for s in range(experts):
            hot = slots == CR[s][0:1, :]
            GS[s, 0:1, :] = jnp.sum(
                jnp.where(hot, score[s * cap : (s + 1) * cap, :], 0.0), axis=0, keepdims=True
            )

        def send(k, carry):
            g_copy((e + k) % experts, e).start()
            return carry

        lax.fori_loop(1, experts, send, 0)
        GR[pl.ds(e, 1)] = GS[pl.ds(e, 1)]

    def release(j):
        slot = pslot(j)
        rc(FYP, j, PB.at[slot, 2:4, opp(y)], FP.at[j], yp).wait_send()
        rc(FYM, j, PB.at[slot, 0:2, opp(y)], FM.at[j], ym).wait_send()
        rc(RYP, j, PB.at[slot, :, up(y)], RP.at[j], yp).wait_send()
        rc(RYM, j, PB.at[slot, :, down(y)], RM.at[j], ym).wait_send()

    def stage_r1(j):
        slot = pslot(j)
        rc(FYP, j, PB.at[slot, 2:4, opp(y)], FP.at[j], yp).wait_recv()
        PB[slot, 2:4, up(y)] = (PB[slot, 2:4, up(y)].astype(F32) + FP[j].astype(F32)).astype(BF16)
        rc(RYP, j, PB.at[slot, :, up(y)], RP.at[j], yp).start()
        rc(FYM, j, PB.at[slot, 0:2, opp(y)], FM.at[j], ym).wait_recv()
        PB[slot, 0:2, down(y)] = (PB[slot, 0:2, down(y)].astype(F32) + FM[j].astype(F32)).astype(BF16)
        rc(RYM, j, PB.at[slot, :, down(y)], RM.at[j], ym).start()

    def stage_r2(j):
        slot = pslot(j)
        rc(RYP, j, PB.at[slot, :, up(y)], RP.at[j], yp).wait_recv()
        rc(RYM, j, PB.at[slot, :, down(y)], RM.at[j], ym).wait_recv()
        S[j] = (PB[slot, :, y].astype(F32) + RP[j].astype(F32) + RM[j].astype(F32)).astype(BF16)
        rc(FZP, j, S.at[j, opp(z), :, 0:half], ZFP.at[j], zp).start()
        rc(FZM, j, S.at[j, opp(z), :, half:C], ZFM.at[j], zm).start()

    def stage_r3(j):
        rc(FZP, j, S.at[j, opp(z), :, 0:half], ZFP.at[j], zp).wait_recv()
        S[j, up(z), :, 0:half] = (S[j, up(z), :, 0:half].astype(F32) + ZFP[j].astype(F32)).astype(BF16)
        rc(RZP, j, S.at[j, up(z)], ZRP.at[j], zp).start()
        rc(FZM, j, S.at[j, opp(z), :, half:C], ZFM.at[j], zm).wait_recv()
        S[j, down(z), :, half:C] = (S[j, down(z), :, half:C].astype(F32) + ZFM[j].astype(F32)).astype(BF16)
        rc(RZM, j, S.at[j, down(z)], ZRM.at[j], zm).start()

    def stage_r4(j):
        rc(RZP, j, S.at[j, up(z)], ZRP.at[j], zp).wait_recv()
        rc(RZM, j, S.at[j, down(z)], ZRM.at[j], zm).wait_recv()
        grad_out[:, cols(j)] = S[j, z].astype(F32) + ZRP[j].astype(F32) + ZRM[j].astype(F32)

    lanes = lax.broadcasted_iota(jnp.int32, (t_dev, experts), 1)
    chosen = jnp.zeros((t_dev, experts), F32)
    for k in range(ids.shape[1]):
        chosen = chosen + jnp.where(ids[:, k : k + 1] == lanes, 1.0, 0.0)
    row = lax.broadcasted_iota(jnp.int32, (t_dev, t_dev), 0)
    col = lax.broadcasted_iota(jnp.int32, (t_dev, t_dev), 1)
    earlier = jnp.where(col < row, 1.0, 0.0).astype(BF16)
    slot_of = jnp.dot(earlier, chosen.astype(BF16), preferred_element_type=F32)
    code = jnp.where(chosen > 0.5, slot_of, -1.0)
    scores = logits[...]
    powers = jnp.exp(scores - jnp.max(scores, axis=1, keepdims=True))
    probs = powers / jnp.sum(powers, axis=1, keepdims=True)
    code_t = code.T
    probs_t = probs.T
    PT[...] = probs_t
    gate_t = probs_t.astype(BF16).astype(F32)
    CS[...] = jnp.zeros_like(CS)
    GS[...] = jnp.zeros_like(GS)
    ACC[...] = jnp.zeros_like(ACC)
    for s in range(experts):
        CS[s, 0:1, :] = code_t[s : s + 1, :]
        CS[s, 1:2, :] = gate_t[s : s + 1, :]

    def send_code(k, carry):
        c_copy((e + k) % experts, e).start()
        return carry

    stage0(0)
    lax.fori_loop(1, experts, send_code, 0)
    HT[...] = hid[...].T

    def tick(i, carry):
        at_stage(i, LAG_C + 1, stage_r1)
        at_stage(i, LAG_C + 2, stage_r2)
        at_stage(i, LAG_C + 3, stage_r3)
        at_stage(i, LAG_C + 4, stage_r4)

        @pl.when(jnp.logical_and(i > 0, i < nc))
        def _():
            stage0(i)

        at_stage(i, 1, stage1)
        at_stage(i, 2, stage2)
        at_stage(i, 3, stage3)
        at_stage(i, LAG_C, stage_c)
        return carry

    lax.fori_loop(0, nc + LAG_C + 4, tick, 0)

    def wait_gain(k, carry):
        peer = (e + k) % experts
        g_copy(peer, peer).wait_recv()
        return carry

    lax.fori_loop(1, experts, wait_gain, 0)
    gain = jnp.concatenate([GR[s][0:1, :] for s in range(experts)], axis=0)
    probs_t = PT[...]
    router_t = probs_t * (gain - jnp.sum(probs_t * gain, axis=0, keepdims=True))
    router_out[...] = router_t.T

    def drain(j, carry):
        ref = block(j, zl, x, core)
        for kind in range(SIB_F + 2):
            rc(kind, j, ref, ref, sib).wait_send()
        ref = W.at[j, z, y]
        for kind in (WZP, WZM, WZF):
            rc(kind, j, ref, ref, zp).wait_send()
        for kind in (WYP, WYM):
            rc(kind, j, W.at[j, :, y], W.at[j, :, y], yp).wait_send()
        for kind in (WYPF, WYMF):
            rc(kind, j, W.at[j, 0:2, y], W.at[j, 0:2, y], yp).wait_send()
        rc(FZP, j, S.at[j, opp(z), :, 0:half], ZFP.at[j], zp).wait_send()
        rc(FZM, j, S.at[j, opp(z), :, half:C], ZFM.at[j], zm).wait_send()
        rc(RZP, j, S.at[j, up(z)], ZRP.at[j], zp).wait_send()
        rc(RZM, j, S.at[j, down(z)], ZRM.at[j], zm).wait_send()

        @pl.when(j >= nc - KEEP)
        def _():
            release(j)

        return carry

    lax.fori_loop(0, nc, drain, 0)

    def drain_small(k, carry):
        peer = (e + k) % experts
        c_copy(peer, e).wait_send()
        g_copy(peer, e).wait_send()
        return carry

    lax.fori_loop(1, experts, drain_small, 0)


def exchange(out_grad, router_logits, choice_ids, saved, weight_low):
    t_dev, width = out_grad.shape
    experts = router_logits.shape[1]
    rows_all, ff = saved.shape
    own = weight_low.shape[0]
    nc = PARTS
    C = width // nc
    vm = pl.BlockSpec(memory_space=pltpu.VMEM)
    hbm = pl.BlockSpec(memory_space=pl.ANY)
    dma = pltpu.SemaphoreType.DMA
    return pl.pallas_call(
        kernel,
        out_shape=(
            jax.ShapeDtypeStruct((own, width), F32),
            jax.ShapeDtypeStruct((t_dev, experts), F32),
        ),
        in_specs=[hbm, vm, vm, vm, hbm],
        out_specs=(vm, vm),
        scratch_shapes=[
            pltpu.VMEM((nc, experts, t_dev, C), BF16),
            pltpu.VMEM((nc, NZ, NY, own, C), BF16),
            pltpu.VMEM((KEEP, NZ, NY, own, C), BF16),
            pltpu.VMEM((nc, 2, own, C), BF16),
            pltpu.VMEM((nc, 2, own, C), BF16),
            pltpu.VMEM((nc, NZ, own, C), BF16),
            pltpu.VMEM((nc, NZ, own, C), BF16),
            pltpu.VMEM((nc, NZ, own, C), BF16),
            pltpu.VMEM((nc, own, C // 2), BF16),
            pltpu.VMEM((nc, own, C // 2), BF16),
            pltpu.VMEM((nc, own, C), BF16),
            pltpu.VMEM((nc, own, C), BF16),
            pltpu.VMEM((ff, rows_all), BF16),
            pltpu.VMEM((experts // 2, 4 * (rows_all // experts), 2 * t_dev), BF16),
            pltpu.VMEM((rows_all, C), BF16),
            pltpu.VMEM((rows_all, C), BF16),
            pltpu.VMEM((rows_all, 128), F32),
            pltpu.VMEM((experts, 8, t_dev), F32),
            pltpu.VMEM((experts, 8, t_dev), F32),
            pltpu.VMEM((experts, 8, t_dev), F32),
            pltpu.VMEM((experts, 8, t_dev), F32),
            pltpu.VMEM((experts, t_dev), F32),
            dma((KINDS, nc)),
            dma((KINDS, nc)),
            dma((nc,)),
            dma((nc,)),
            dma((experts,)),
            dma((experts,)),
            dma((experts,)),
            dma((experts,)),
        ],
        compiler_params=pltpu.CompilerParams(
            collective_id=0, has_side_effects=True, vmem_limit_bytes=62 * 1024 * 1024
        ),
    )(out_grad, choice_ids, router_logits, saved, weight_low)


def shards(out_grad, router_logits, choice_ids, hidden, master, first, second):
    own, _, width = master.shape
    saved = hidden.reshape(hidden.shape[2] * hidden.shape[3], hidden.shape[4])
    weight_low = master.astype(BF16).reshape(own, width)
    grad, router_grad = exchange(out_grad, router_logits, choice_ids, saved, weight_low)
    grad = grad.reshape(own, 1, width)
    new_first = beta_one * first + (1.0 - beta_one) * grad
    new_second = beta_two * second + (1.0 - beta_two) * grad * grad
    first_hat = new_first / (1.0 - beta_one**adam_step)
    second_hat = new_second / (1.0 - beta_two**adam_step)
    new_weight = master - learn_rate * (
        first_hat / (jnp.sqrt(second_hat) + epsilon) + decay_rate * master
    )
    return (new_weight, new_first, new_second, router_grad)


def solution(mesh):
    return jax.shard_map(
        shards,
        mesh=mesh,
        in_specs=(
            P(("dp", "expert"), None),
            P(("dp", "expert"), None),
            P(("dp", "expert"), None),
            P("dp", "expert", None, None, None),
            P("dp", "expert", None),
            P("dp", "expert", None),
            P("dp", "expert", None),
        ),
        out_specs=(
            P("dp", "expert", None),
            P("dp", "expert", None),
            P("dp", "expert", None),
            P(("dp", "expert"), None),
        ),
        check_vma=False,
    )
```

```python
import functools

import jax
import jax.numpy as jnp
from jax import lax
from jax.experimental import pallas as pl
from jax.experimental.pallas import tpu as pltpu
from jax.sharding import PartitionSpec as P

beta_one = 0.9
beta_two = 0.95
learn_rate = 0.001
decay_rate = 0.1
epsilon = 1e-08
adam_step = 100.0

MESH = pl.DeviceIdType.MESH
F32 = jnp.float32
BF16 = jnp.bfloat16

NZ, NY, NX = 4, 4, 4
PARTS = 20
HOP = 2
KEEP = 2 * HOP + 2

Z_OWN, XP_OWN, XM_OWN, SIB_OWN = 0, 1, 2, 3
XP_PART, XM_PART, SIB_PART = 4, 5, 6
XP_FWD, XM_FWD = 7, 8
SIB_X = 9
SIB_F = 13
WZ, WZF, WY, WYF, SF, SR = 15, 16, 17, 18, 19, 20
SENDS = 21

(R_Z, R_X, R_XF, R_SIB, R_WZ, R_WZF, R_WY, R_WYF, R_FY, R_RY, R_FZ, R_RZ) = range(12)
RECVS = 12


def kernel(
    og, ids, logits, hid_in, master_in, grad_out, router_out,
    G, W, PB, FY, RY, S, FZ, RZ,
    hid, master, HT, OH, ROWS, SCALED, ACC, CS, CR, GS, GR, PT,
    ss, rs, ps, l1, l2, cs_s, cs_r, gs_s, gs_r,
):
    nc, experts, t_dev, C = G.shape
    rows_all, ff = hid.shape
    cap = rows_all // experts
    half = C // 2
    d = lax.axis_index("dp")
    e = lax.axis_index("expert")
    z, y = d // NY, d % NY
    zl, x, core = e // (2 * NX), (e // 2) % NX, e % 2
    up = lambda v: (v + 1) % 4
    down = lambda v: (v + 3) % 4
    opp = lambda v: (v + 2) % 4
    eid = lambda a, b, c: a * (2 * NX) + b * 2 + c
    did = lambda a, b: a * NY + b

    part = (d, eid(1 - zl, x, core))
    xp = (d, eid(zl, up(x), core))
    xm = (d, eid(zl, down(x), core))
    sib = (d, eid(zl, x, 1 - core))
    zp = (did(up(z), y), e)
    zm = (did(down(z), y), e)
    yp = (did(z, up(y)), e)
    ym = (did(z, down(y)), e)

    def rc(send, recv, src, dst, dev):
        return pltpu.make_async_remote_copy(
            src_ref=src, dst_ref=dst, send_sem=send, recv_sem=recv, device_id=dev, device_id_type=MESH
        )

    def arrive(recv, j, ref):
        rc(ss.at[0], rs.at[recv, j], ref, ref, sib).wait_recv()

    def left(send, ref):
        rc(send, rs.at[0, 0], ref, ref, sib).wait_send()

    def cols(j, width=C):
        return pl.ds(pl.multiple_of(j * C, C), width)

    def local_g(j):
        return pltpu.make_async_copy(og.at[:, cols(j)], G.at[j, e], l1.at[j])

    own, lanes_of = W.shape[3], nc * C // 128

    def flat(j, k):
        return pl.ds(j * (C // 128) + k, own, stride=lanes_of)

    def stage_local(j, carry):
        local_g(j).start()
        return carry

    load_master = pltpu.make_async_copy(master_in, master, l2.at[0])
    load_hidden = pltpu.make_async_copy(hid_in, hid, l2.at[1])
    load_master.start()
    lax.fori_loop(0, nc, stage_local, 0)
    load_hidden.start()

    barrier = pltpu.get_barrier_semaphore()

    def greet(k, carry):
        pl.semaphore_signal(barrier, inc=1, device_id=(d, (e + k) % experts), device_id_type=MESH)
        return carry

    lax.fori_loop(1, experts, greet, 0)
    for dev in (zp, zm, yp, ym):
        pl.semaphore_signal(barrier, inc=1, device_id=dev, device_id_type=MESH)
    pl.semaphore_wait(barrier, experts - 1 + 4)

    def send_d(kind, recv, j, a, b, dev):
        ref = G.at[j, eid(a, b, core)]
        rc(ss.at[kind], rs.at[recv, j], ref, ref, dev).start()

    def send_w(kind, recv, j, ref, dev):
        rc(ss.at[kind], rs.at[recv, j], ref, ref, dev).start()

    def pslot(j):
        return j % KEEP

    def c_copy(peer, source):
        return pltpu.make_async_remote_copy(
            src_ref=CS.at[peer], dst_ref=CR.at[source], send_sem=cs_s.at[peer], recv_sem=cs_r.at[source],
            device_id=(d, peer), device_id_type=MESH,
        )

    def g_copy(peer, source):
        return pltpu.make_async_remote_copy(
            src_ref=GS.at[peer], dst_ref=GR.at[source], send_sem=gs_s.at[peer], recv_sem=gs_r.at[source],
            device_id=(d, peer), device_id_type=MESH,
        )

    def at_stage(i, lag, fn):
        j = i - lag

        @pl.when(jnp.logical_and(j >= 0, j < nc))
        def _():
            fn(j)

    def stage0(j):
        local_g(j).wait()
        for k in range(C // 128):
            W[j, z, y, :, k * 128 : (k + 1) * 128] = master[flat(j, k), :].astype(BF16)
        send_d(Z_OWN, R_Z, j, zl, x, part)
        send_d(XP_OWN, R_X, j, zl, x, xp)
        send_d(XM_OWN, R_X, j, zl, x, xm)
        send_d(SIB_OWN, R_SIB, j, zl, x, sib)
        send_w(WZ, R_WZ, j, W.at[j, z, y], zp)
        send_w(WZ, R_WZ, j, W.at[j, z, y], zm)

    def stage1(j):
        arrive(R_Z, j, G.at[j, 0])
        send_d(XP_PART, R_X, j, 1 - zl, x, xp)
        send_d(XM_PART, R_X, j, 1 - zl, x, xm)
        send_d(SIB_PART, R_SIB, j, 1 - zl, x, sib)
        arrive(R_WZ, j, W.at[j, 0, 0:2])

        @pl.when(j % 2 == 0)
        def _():
            send_w(WZF, R_WZF, j, W.at[j, down(z), y], zp)

        @pl.when(j % 2 == 1)
        def _():
            send_w(WZF, R_WZF, j, W.at[j, up(z), y], zm)

    def stage2(j):
        arrive(R_X, j, G.at[j, 0:4])
        send_d(XP_FWD, R_XF, j, 0, down(x), xp)
        send_d(XM_FWD, R_XF, j, 1, up(x), xm)
        arrive(R_WZF, j, W.at[j, 0, 0])
        send_w(WY, R_WY, j, W.at[j, :, y], yp)
        send_w(WY, R_WY, j, W.at[j, :, y], ym)
        for k, (a, b) in enumerate(((0, down(x)), (1, down(x)), (0, up(x)), (1, up(x)))):
            send_d(SIB_X + k, R_SIB, j, a, b, sib)

    def stage3(j):
        arrive(R_WY, j, W.at[j, 0:2])
        send_w(WYF, R_WYF, j, W.at[j, 0:2, down(y)], yp)
        send_w(WYF, R_WYF, j, W.at[j, 2:4, up(y)], ym)
        arrive(R_XF, j, G.at[j, 0:2])
        for k in range(2):
            send_d(SIB_F + k, R_SIB, j, k, opp(x), sib)

    def setup_select():
        def wait_code(k, carry):
            c_copy((e + k) % experts, (e + k) % experts).wait_recv()
            return carry

        lax.fori_loop(1, experts, wait_code, 0)
        CR[pl.ds(e, 1)] = CS[pl.ds(e, 1)]
        slots = lax.broadcasted_iota(jnp.int32, (cap, t_dev), 0).astype(F32)
        empty = jnp.zeros((cap, t_dev), F32)
        for p in range(experts // 2):
            one, weighted = [], []
            for s in range(2):
                tile = CR[2 * p + s]
                hot = jnp.where(slots == tile[0:1, :], 1.0, 0.0)
                gate = hot * tile[1:2, :]
                one.append(jnp.concatenate([hot, empty] if s == 0 else [empty, hot], axis=1))
                weighted.append(jnp.concatenate([gate, empty] if s == 0 else [empty, gate], axis=1))
            OH[p] = jnp.concatenate(one + weighted, axis=0).astype(BF16)

    def stage_c(j):
        @pl.when(j == 0)
        def _():
            setup_select()

        arrive(R_SIB, j, G.at[j, 0:8])

        pair = 2 * cap
        for p in range(experts // 2):
            tokens = G[j, 2 * p : 2 * p + 2].reshape(2 * t_dev, C)
            picked = jnp.dot(OH[p], tokens, preferred_element_type=F32)
            ROWS[p * pair : (p + 1) * pair, :] = picked[:pair].astype(BF16)
            SCALED[p * pair : (p + 1) * pair, :] = picked[pair:].astype(BF16)

        slot = pslot(j)

        @pl.when(j >= KEEP)
        def _():
            release(j - KEEP)

        partial = jnp.dot(HT[...], SCALED[...], preferred_element_type=F32)
        PB[slot] = partial.astype(BF16).reshape(NZ, NY, ff // (NZ * NY), C)
        rc(ps.at[slot], rs.at[R_FY, j], PB.at[slot, 2:4, opp(y)], FY.at[j, 0], yp).start()
        rc(ps.at[slot], rs.at[R_FY, j], PB.at[slot, 0:2, opp(y)], FY.at[j, 1], ym).start()

        arrive(R_WYF, j, W.at[j, 0])
        through = jnp.dot(hid[...], W[j].reshape(ff, C), preferred_element_type=F32)
        product = through * ROWS[...].astype(F32)
        total = product[:, 0:128]
        for k in range(1, C // 128):
            total = total + product[:, k * 128 : (k + 1) * 128]
        ACC[...] += total

        @pl.when(j == nc - 1)
        def _():
            send_scores()

    def send_scores():
        score = jnp.sum(ACC[...], axis=1, keepdims=True)
        slots = lax.broadcasted_iota(jnp.int32, (cap, t_dev), 0).astype(F32)
        for s in range(experts):
            hot = slots == CR[s][0:1, :]
            GS[s, 0:1, :] = jnp.sum(
                jnp.where(hot, score[s * cap : (s + 1) * cap, :], 0.0), axis=0, keepdims=True
            )

        def send(k, carry):
            g_copy((e + k) % experts, e).start()
            return carry

        lax.fori_loop(1, experts, send, 0)
        GR[pl.ds(e, 1)] = GS[pl.ds(e, 1)]

    def release(j):
        slot = pslot(j)
        left(ps.at[slot], PB.at[slot, 0:3])

    def add(a, b):
        return (a.astype(F32) + b.astype(F32)).astype(BF16)

    def stage_r1(j):
        slot = pslot(j)
        arrive(R_FY, j, FY.at[j])
        PB[slot, 2:4, up(y)] = add(PB[slot, 2:4, up(y)], FY[j, 0])
        rc(ps.at[slot], rs.at[R_RY, j], PB.at[slot, :, up(y)], RY.at[j, 0], yp).start()
        PB[slot, 0:2, down(y)] = add(PB[slot, 0:2, down(y)], FY[j, 1])
        rc(ps.at[slot], rs.at[R_RY, j], PB.at[slot, :, down(y)], RY.at[j, 1], ym).start()

    def stage_r2(j):
        slot = pslot(j)
        arrive(R_RY, j, RY.at[j])
        S[j] = (PB[slot, :, y].astype(F32) + RY[j, 0].astype(F32) + RY[j, 1].astype(F32)).astype(BF16)
        rc(ss.at[SF], rs.at[R_FZ, j], S.at[j, opp(z), :, 0:half], FZ.at[j, 0], zp).start()
        rc(ss.at[SF], rs.at[R_FZ, j], S.at[j, opp(z), :, half:C], FZ.at[j, 1], zm).start()

    def stage_r3(j):
        arrive(R_FZ, j, FZ.at[j])
        S[j, up(z), :, 0:half] = add(S[j, up(z), :, 0:half], FZ[j, 0])
        rc(ss.at[SR], rs.at[R_RZ, j], S.at[j, up(z)], RZ.at[j, 0], zp).start()
        S[j, down(z), :, half:C] = add(S[j, down(z), :, half:C], FZ[j, 1])
        rc(ss.at[SR], rs.at[R_RZ, j], S.at[j, down(z)], RZ.at[j, 1], zm).start()

    def stage_r4(j):
        arrive(R_RZ, j, RZ.at[j])
        total = S[j, z].astype(F32) + RZ[j, 0].astype(F32) + RZ[j, 1].astype(F32)
        for k in range(C // 128):
            grad_out[flat(j, k), :] = total[:, k * 128 : (k + 1) * 128]

    labels = lax.broadcasted_iota(jnp.int32, (experts, t_dev), 0)
    chosen = jnp.zeros((experts, t_dev), F32)
    for k in range(ids.shape[0]):
        chosen = chosen + jnp.where(ids[k : k + 1, :] == labels, 1.0, 0.0)
    row = lax.broadcasted_iota(jnp.int32, (t_dev, t_dev), 0)
    col = lax.broadcasted_iota(jnp.int32, (t_dev, t_dev), 1)
    earlier = jnp.where(row < col, 1.0, 0.0).astype(BF16)
    slot_of = jnp.dot(chosen.astype(BF16), earlier, preferred_element_type=F32)
    code_t = jnp.where(chosen > 0.5, slot_of, -1.0)
    scores = logits[...]
    powers = jnp.exp(scores - jnp.max(scores, axis=0, keepdims=True))
    probs_t = powers / jnp.sum(powers, axis=0, keepdims=True)
    PT[...] = probs_t
    gate_t = probs_t.astype(BF16).astype(F32)
    CS[...] = jnp.zeros_like(CS)
    GS[...] = jnp.zeros_like(GS)
    ACC[...] = jnp.zeros_like(ACC)
    for s in range(experts):
        CS[s, 0:1, :] = code_t[s : s + 1, :]
        CS[s, 1:2, :] = gate_t[s : s + 1, :]

    def send_code(k, carry):
        c_copy((e + k) % experts, e).start()
        return carry

    load_master.wait()
    stage0(0)
    lax.fori_loop(1, experts, send_code, 0)
    load_hidden.wait()
    HT[...] = hid[...].T

    def tick(i, carry):
        at_stage(i, 5 * HOP, stage_r1)
        at_stage(i, 6 * HOP, stage_r2)
        at_stage(i, 7 * HOP, stage_r3)
        at_stage(i, 8 * HOP, stage_r4)

        @pl.when(jnp.logical_and(i > 0, i < nc))
        def _():
            stage0(i)

        at_stage(i, HOP, stage1)
        at_stage(i, 2 * HOP, stage2)
        at_stage(i, 3 * HOP, stage3)
        at_stage(i, 4 * HOP, stage_c)
        return carry

    lax.fori_loop(0, nc + 8 * HOP, tick, 0)

    def wait_gain(k, carry):
        peer = (e + k) % experts
        g_copy(peer, peer).wait_recv()
        return carry

    lax.fori_loop(1, experts, wait_gain, 0)
    gain = jnp.concatenate([GR[s][0:1, :] for s in range(experts)], axis=0)
    probs_t = PT[...]
    router_out[...] = probs_t * (gain - jnp.sum(probs_t * gain, axis=0, keepdims=True))

    for kind in range(SIB_F + 2):
        left(ss.at[kind], G.at[:, kind])
    left(ss.at[WZ], W.at[:, 0, 0:2])
    left(ss.at[WZF], W.at[:, 0, 0])
    left(ss.at[WY], W.at[:, 0:2])
    left(ss.at[WYF], W.at[:, 0])
    left(ss.at[SF], S.at[:, 0])
    left(ss.at[SR], S.at[:, 0:2])
    for j in range(nc - KEEP, nc):
        release(j)

    def drain_small(k, carry):
        peer = (e + k) % experts
        c_copy(peer, e).wait_send()
        g_copy(peer, e).wait_send()
        return carry

    lax.fori_loop(1, experts, drain_small, 0)


def exchange(out_grad, logits, choices, saved, master):
    t_dev, width = out_grad.shape
    experts = logits.shape[0]
    rows_all, ff = saved.shape
    own = master.shape[0] * 128 // width
    nc = PARTS
    C = width // nc
    vm = pl.BlockSpec(memory_space=pltpu.VMEM)
    hbm = pl.BlockSpec(memory_space=pl.ANY)
    dma = pltpu.SemaphoreType.DMA
    return pl.pallas_call(
        kernel,
        out_shape=(
            jax.ShapeDtypeStruct(master.shape, F32),
            jax.ShapeDtypeStruct((experts, t_dev), F32),
        ),
        in_specs=[hbm, vm, vm, hbm, hbm],
        out_specs=(vm, vm),
        scratch_shapes=[
            pltpu.VMEM((nc, experts, t_dev, C), BF16),
            pltpu.VMEM((nc, NZ, NY, own, C), BF16),
            pltpu.VMEM((KEEP, NZ, NY, own, C), BF16),
            pltpu.VMEM((nc, 2, 2, own, C), BF16),
            pltpu.VMEM((nc, 2, NZ, own, C), BF16),
            pltpu.VMEM((nc, NZ, own, C), BF16),
            pltpu.VMEM((nc, 2, own, C // 2), BF16),
            pltpu.VMEM((nc, 2, own, C), BF16),
            pltpu.VMEM(saved.shape, BF16),
            pltpu.VMEM(master.shape, F32),
            pltpu.VMEM((ff, rows_all), BF16),
            pltpu.VMEM((experts // 2, 4 * (rows_all // experts), 2 * t_dev), BF16),
            pltpu.VMEM((rows_all, C), BF16),
            pltpu.VMEM((rows_all, C), BF16),
            pltpu.VMEM((rows_all, 128), F32),
            pltpu.VMEM((experts, 8, t_dev), F32),
            pltpu.VMEM((experts, 8, t_dev), F32),
            pltpu.VMEM((experts, 8, t_dev), F32),
            pltpu.VMEM((experts, 8, t_dev), F32),
            pltpu.VMEM((experts, t_dev), F32),
            dma((SENDS,)),
            dma((RECVS, nc)),
            dma((KEEP,)),
            dma((nc,)),
            dma((2,)),
            dma((experts,)),
            dma((experts,)),
            dma((experts,)),
            dma((experts,)),
        ],
        compiler_params=pltpu.CompilerParams(
            collective_id=0, has_side_effects=True, vmem_limit_bytes=62 * 1024 * 1024
        ),
    )(out_grad, choices, logits, saved, master)


def shards(out_grad, router_logits, choice_ids, hidden, master, first, second):
    saved = hidden.reshape(hidden.shape[2] * hidden.shape[3], hidden.shape[4])
    grad, router_grad = exchange(
        out_grad, router_logits.T, choice_ids.T, saved, master.reshape(-1, 128)
    )
    grad = grad.reshape(master.shape)
    new_first = beta_one * first + (1.0 - beta_one) * grad
    new_second = beta_two * second + (1.0 - beta_two) * grad * grad
    first_hat = new_first / (1.0 - beta_one**adam_step)
    second_hat = new_second / (1.0 - beta_two**adam_step)
    new_weight = master - learn_rate * (
        first_hat / (jnp.sqrt(second_hat) + epsilon) + decay_rate * master
    )
    return (new_weight, new_first, new_second, router_grad.T)


def solution(mesh):
    return jax.shard_map(
        shards,
        mesh=mesh,
        in_specs=(
            P(("dp", "expert"), None),
            P(("dp", "expert"), None),
            P(("dp", "expert"), None),
            P("dp", "expert", None, None, None),
            P("dp", "expert", None),
            P("dp", "expert", None),
            P("dp", "expert", None),
        ),
        out_specs=(
            P("dp", "expert", None),
            P("dp", "expert", None),
            P("dp", "expert", None),
            P(("dp", "expert"), None),
        ),
        check_vma=False,
    )
```

```python
import functools

import jax
import jax.numpy as jnp
from jax import lax
from jax.experimental import pallas as pl
from jax.experimental.pallas import tpu as pltpu
from jax.sharding import PartitionSpec as P

beta_one = 0.9
beta_two = 0.95
learn_rate = 0.001
decay_rate = 0.1
epsilon = 1e-08
adam_step = 100.0

MESH = pl.DeviceIdType.MESH
F32 = jnp.float32
BF16 = jnp.bfloat16

NZ, NY, NX = 4, 4, 4
PARTS = 20
HOP = 2
KEEP = 2 * HOP + 2
Y_FIRST = 5
STRAIGHT = 3

Z_OWN, XP_OWN, XM_OWN, SIB_OWN = 0, 1, 2, 3
XP_PART, XM_PART, SIB_PART = 4, 5, 6
XP_FWD, XM_FWD = 7, 8
SIB_X = 9
SIB_F = 13
WZ, WZF, WY, WYF, SF, SR = 15, 16, 17, 18, 19, 20
SENDS = 21

(R_Z, R_X, R_XF, R_SIB, R_WZ, R_WZF, R_WY, R_WYF, R_FY, R_RY, R_FZ, R_RZ) = range(12)
RECVS = 12


def kernel(
    og, ids, logits, hid_in, master_in, grad_out, router_out,
    G, W, PB, FY, RY, S, FZ, RZ,
    hid, master, HT, OH, ROWS, SCALED, ACC, CS, CR, GS, GR, PT,
    ss, rs, ps, l1, l2, cs_s, cs_r, gs_s, gs_r,
):
    nc, experts, t_dev, C = G.shape
    rows_all, ff = hid.shape
    cap = rows_all // experts
    half = C // 2
    d = lax.axis_index("dp")
    e = lax.axis_index("expert")
    z, y = d // NY, d % NY
    zl, x, core = e // (2 * NX), (e // 2) % NX, e % 2
    up = lambda v: (v + 1) % 4
    down = lambda v: (v + 3) % 4
    opp = lambda v: (v + 2) % 4
    eid = lambda a, b, c: a * (2 * NX) + b * 2 + c
    did = lambda a, b: a * NY + b

    part = (d, eid(1 - zl, x, core))
    xp = (d, eid(zl, up(x), core))
    xm = (d, eid(zl, down(x), core))
    sib = (d, eid(zl, x, 1 - core))
    zp = (did(up(z), y), e)
    zm = (did(down(z), y), e)
    yp = (did(z, up(y)), e)
    ym = (did(z, down(y)), e)
    zo = (did(opp(z), y), e)

    def rc(send, recv, src, dst, dev):
        return pltpu.make_async_remote_copy(
            src_ref=src, dst_ref=dst, send_sem=send, recv_sem=recv, device_id=dev, device_id_type=MESH
        )

    def arrive(recv, j, ref):
        rc(ss.at[0], rs.at[recv, j], ref, ref, sib).wait_recv()

    def left(send, ref):
        rc(send, rs.at[0, 0], ref, ref, sib).wait_send()

    def cols(j, width=C):
        return pl.ds(pl.multiple_of(j * C, C), width)

    def local_g(j):
        return pltpu.make_async_copy(og.at[:, cols(j)], G.at[j, e], l1.at[j])

    own, lanes_of = W.shape[3], nc * C // 128

    def flat(j, k):
        return pl.ds(j * (C // 128) + k, own, stride=lanes_of)

    def stage_local(j, carry):
        local_g(j).start()
        return carry

    load_master = pltpu.make_async_copy(master_in, master, l2.at[0])
    load_hidden = pltpu.make_async_copy(hid_in, hid, l2.at[1])
    load_master.start()
    lax.fori_loop(0, nc, stage_local, 0)
    load_hidden.start()

    barrier = pltpu.get_barrier_semaphore()

    def greet(k, carry):
        pl.semaphore_signal(barrier, inc=1, device_id=(d, (e + k) % experts), device_id_type=MESH)
        return carry

    lax.fori_loop(1, experts, greet, 0)
    for dev in (zp, zm, yp, ym):
        pl.semaphore_signal(barrier, inc=1, device_id=dev, device_id_type=MESH)
    pl.semaphore_wait(barrier, experts - 1 + 4)

    def send_d(kind, recv, j, a, b, dev):
        ref = G.at[j, eid(a, b, core)]
        rc(ss.at[kind], rs.at[recv, j], ref, ref, dev).start()

    def send_w(kind, recv, j, ref, dev):
        rc(ss.at[kind], rs.at[recv, j], ref, ref, dev).start()

    def pslot(j):
        return j % KEEP

    def c_copy(peer, source):
        return pltpu.make_async_remote_copy(
            src_ref=CS.at[peer], dst_ref=CR.at[source], send_sem=cs_s.at[peer], recv_sem=cs_r.at[source],
            device_id=(d, peer), device_id_type=MESH,
        )

    def g_copy(peer, source):
        return pltpu.make_async_remote_copy(
            src_ref=GS.at[peer], dst_ref=GR.at[source], send_sem=gs_s.at[peer], recv_sem=gs_r.at[source],
            device_id=(d, peer), device_id_type=MESH,
        )

    def at_stage(i, lag, fn):
        j = i - lag

        @pl.when(jnp.logical_and(j >= 0, j < nc))
        def _():
            fn(j)

    def weights_by_order(j, send):
        turned = j % Y_FIRST == Y_FIRST - 1

        @pl.when(turned)
        def _():
            send(j, True)

        @pl.when(jnp.logical_not(turned))
        def _():
            send(j, False)

    def place(j, a, b, y_first):
        return W.at[j, b, a] if y_first else W.at[j, a, b]

    def weights0(j, y_first):
        ref = W.at[j, z, y]
        for dev in (yp, ym) if y_first else (zp, zm):
            send_w(WZ, R_WZ, j, ref, dev)
        for dev in (zp, zm) if y_first else (yp, ym):
            send_w(WY, R_WY, j, ref, dev)

    def weights1(j, y_first):
        a, b = (y, z) if y_first else (z, y)
        before, after = place(j, down(a), b, y_first), place(j, up(a), b, y_first)
        ahead, back = (yp, ym) if y_first else (zp, zm)

        @pl.when(j % 2 == 0)
        def _():
            send_w(WZF, R_WZF, j, before, ahead)

        @pl.when(j % 2 == 1)
        def _():
            send_w(WZF, R_WZF, j, after, back)

        for dev in (zp, zm) if y_first else (yp, ym):
            send_w(WY, R_WY, j, before, dev)
            send_w(WY, R_WY, j, after, dev)

    def weights2(j, y_first):
        a, b = (y, z) if y_first else (z, y)
        for dev in (zp, zm) if y_first else (yp, ym):
            send_w(WY, R_WY, j, place(j, opp(a), b, y_first), dev)

    def weights3(j, y_first):
        if y_first:
            send_w(WYF, R_WYF, j, W.at[j, down(z), 0:2], zp)
            send_w(WYF, R_WYF, j, W.at[j, up(z), 2:4], zm)
        else:
            send_w(WYF, R_WYF, j, W.at[j, 0:2, down(y)], yp)
            send_w(WYF, R_WYF, j, W.at[j, 2:4, up(y)], ym)

    def stage0(j):
        local_g(j).wait()
        for k in range(C // 128):
            W[j, z, y, :, k * 128 : (k + 1) * 128] = master[flat(j, k), :].astype(BF16)
        send_d(Z_OWN, R_Z, j, zl, x, part)
        send_d(XP_OWN, R_X, j, zl, x, xp)
        send_d(XM_OWN, R_X, j, zl, x, xm)
        send_d(SIB_OWN, R_SIB, j, zl, x, sib)
        weights_by_order(j, weights0)

    def stage1(j):
        arrive(R_Z, j, G.at[j, 0])
        send_d(XP_PART, R_X, j, 1 - zl, x, xp)
        send_d(XM_PART, R_X, j, 1 - zl, x, xm)
        send_d(SIB_PART, R_SIB, j, 1 - zl, x, sib)
        arrive(R_WZ, j, W.at[j, 0, 0:2])
        weights_by_order(j, weights1)

    def stage2(j):
        arrive(R_X, j, G.at[j, 0:4])
        send_d(XP_FWD, R_XF, j, 0, down(x), xp)
        send_d(XM_FWD, R_XF, j, 1, up(x), xm)
        arrive(R_WZF, j, W.at[j, 0, 0])
        weights_by_order(j, weights2)
        for k, (a, b) in enumerate(((0, down(x)), (1, down(x)), (0, up(x)), (1, up(x)))):
            send_d(SIB_X + k, R_SIB, j, a, b, sib)

    def stage3(j):
        arrive(R_WY, j, W.at[j, 0:2])
        weights_by_order(j, weights3)
        arrive(R_XF, j, G.at[j, 0:2])
        for k in range(2):
            send_d(SIB_F + k, R_SIB, j, k, opp(x), sib)

    def setup_select():
        def wait_code(k, carry):
            c_copy((e + k) % experts, (e + k) % experts).wait_recv()
            return carry

        lax.fori_loop(1, experts, wait_code, 0)
        CR[pl.ds(e, 1)] = CS[pl.ds(e, 1)]
        slots = lax.broadcasted_iota(jnp.int32, (cap, t_dev), 0).astype(F32)
        empty = jnp.zeros((cap, t_dev), F32)
        for p in range(experts // 2):
            one, weighted = [], []
            for s in range(2):
                tile = CR[2 * p + s]
                hot = jnp.where(slots == tile[0:1, :], 1.0, 0.0)
                gate = hot * tile[1:2, :]
                one.append(jnp.concatenate([hot, empty] if s == 0 else [empty, hot], axis=1))
                weighted.append(jnp.concatenate([gate, empty] if s == 0 else [empty, gate], axis=1))
            OH[p] = jnp.concatenate(one + weighted, axis=0).astype(BF16)

    def stage_c(j):
        @pl.when(j == 0)
        def _():
            setup_select()

        arrive(R_SIB, j, G.at[j, 0:8])

        pair = 2 * cap
        for p in range(experts // 2):
            tokens = G[j, 2 * p : 2 * p + 2].reshape(2 * t_dev, C)
            picked = jnp.dot(OH[p], tokens, preferred_element_type=F32)
            ROWS[p * pair : (p + 1) * pair, :] = picked[:pair].astype(BF16)
            SCALED[p * pair : (p + 1) * pair, :] = picked[pair:].astype(BF16)

        slot = pslot(j)

        @pl.when(j >= KEEP)
        def _():
            release(j - KEEP)

        partial = jnp.dot(HT[...], SCALED[...], preferred_element_type=F32)
        PB[slot] = partial.astype(BF16).reshape(NZ, NY, ff // (NZ * NY), C)
        rc(ps.at[slot], rs.at[R_FY, j], PB.at[slot, 2:4, opp(y)], FY.at[j, 0], yp).start()
        rc(ps.at[slot], rs.at[R_FY, j], PB.at[slot, 0:2, opp(y)], FY.at[j, 1], ym).start()

        arrive(R_WYF, j, W.at[j, 0])
        through = jnp.dot(hid[...], W[j].reshape(ff, C), preferred_element_type=F32)
        product = through * ROWS[...].astype(F32)
        total = product[:, 0:128]
        for k in range(1, C // 128):
            total = total + product[:, k * 128 : (k + 1) * 128]
        ACC[...] += total

        @pl.when(j == nc - 1)
        def _():
            send_scores()

    def send_scores():
        score = jnp.sum(ACC[...], axis=1, keepdims=True)
        slots = lax.broadcasted_iota(jnp.int32, (cap, t_dev), 0).astype(F32)
        for s in range(experts):
            hot = slots == CR[s][0:1, :]
            GS[s, 0:1, :] = jnp.sum(
                jnp.where(hot, score[s * cap : (s + 1) * cap, :], 0.0), axis=0, keepdims=True
            )

        def send(k, carry):
            g_copy((e + k) % experts, e).start()
            return carry

        lax.fori_loop(1, experts, send, 0)
        GR[pl.ds(e, 1)] = GS[pl.ds(e, 1)]

    def release(j):
        slot = pslot(j)
        left(ps.at[slot], PB.at[slot, 0:3])

    def add(a, b):
        return (a.astype(F32) + b.astype(F32)).astype(BF16)

    def stage_r1(j):
        slot = pslot(j)
        arrive(R_FY, j, FY.at[j])
        PB[slot, 2:4, up(y)] = add(PB[slot, 2:4, up(y)], FY[j, 0])
        rc(ps.at[slot], rs.at[R_RY, j], PB.at[slot, :, up(y)], RY.at[j, 0], yp).start()
        PB[slot, 0:2, down(y)] = add(PB[slot, 0:2, down(y)], FY[j, 1])
        rc(ps.at[slot], rs.at[R_RY, j], PB.at[slot, :, down(y)], RY.at[j, 1], ym).start()

    def stage_r2(j):
        slot = pslot(j)
        arrive(R_RY, j, RY.at[j])
        S[j] = (PB[slot, :, y].astype(F32) + RY[j, 0].astype(F32) + RY[j, 1].astype(F32)).astype(BF16)

        @pl.when(j < nc - STRAIGHT)
        def _():
            rc(ss.at[SF], rs.at[R_FZ, j], S.at[j, opp(z), :, 0:half], FZ.at[j, 0], zp).start()
            rc(ss.at[SF], rs.at[R_FZ, j], S.at[j, opp(z), :, half:C], FZ.at[j, 1], zm).start()

        @pl.when(j >= nc - STRAIGHT)
        def _():
            rc(ss.at[SF], rs.at[R_RZ, j], S.at[j, opp(z)], RZ.at[j, 2], zo).start()
            rc(ss.at[SR], rs.at[R_RZ, j], S.at[j, up(z)], RZ.at[j, 0], zp).start()
            rc(ss.at[SR], rs.at[R_RZ, j], S.at[j, down(z)], RZ.at[j, 1], zm).start()

    def stage_r3(j):
        @pl.when(j < nc - STRAIGHT)
        def _():
            arrive(R_FZ, j, FZ.at[j])
            S[j, up(z), :, 0:half] = add(S[j, up(z), :, 0:half], FZ[j, 0])
            rc(ss.at[SR], rs.at[R_RZ, j], S.at[j, up(z)], RZ.at[j, 0], zp).start()
            S[j, down(z), :, half:C] = add(S[j, down(z), :, half:C], FZ[j, 1])
            rc(ss.at[SR], rs.at[R_RZ, j], S.at[j, down(z)], RZ.at[j, 1], zm).start()

    def stage_r4(j):
        @pl.when(j < nc - STRAIGHT)
        def _():
            arrive(R_RZ, j, RZ.at[j, 0:2])
            store(j, S[j, z].astype(F32) + RZ[j, 0].astype(F32) + RZ[j, 1].astype(F32))

        @pl.when(j >= nc - STRAIGHT)
        def _():
            arrive(R_RZ, j, RZ.at[j])
            store(j, S[j, z].astype(F32) + RZ[j, 0].astype(F32) + RZ[j, 1].astype(F32) + RZ[j, 2].astype(F32))

    def store(j, total):
        for k in range(C // 128):
            grad_out[flat(j, k), :] = total[:, k * 128 : (k + 1) * 128]

    labels = lax.broadcasted_iota(jnp.int32, (experts, t_dev), 0)
    chosen = jnp.zeros((experts, t_dev), F32)
    for k in range(ids.shape[0]):
        chosen = chosen + jnp.where(ids[k : k + 1, :] == labels, 1.0, 0.0)
    row = lax.broadcasted_iota(jnp.int32, (t_dev, t_dev), 0)
    col = lax.broadcasted_iota(jnp.int32, (t_dev, t_dev), 1)
    earlier = jnp.where(row < col, 1.0, 0.0).astype(BF16)
    slot_of = jnp.dot(chosen.astype(BF16), earlier, preferred_element_type=F32)
    code_t = jnp.where(chosen > 0.5, slot_of, -1.0)
    scores = logits[...]
    powers = jnp.exp(scores - jnp.max(scores, axis=0, keepdims=True))
    probs_t = powers / jnp.sum(powers, axis=0, keepdims=True)
    PT[...] = probs_t
    gate_t = probs_t.astype(BF16).astype(F32)
    CS[...] = jnp.zeros_like(CS)
    GS[...] = jnp.zeros_like(GS)
    ACC[...] = jnp.zeros_like(ACC)
    for s in range(experts):
        CS[s, 0:1, :] = code_t[s : s + 1, :]
        CS[s, 1:2, :] = gate_t[s : s + 1, :]

    def send_code(k, carry):
        c_copy((e + k) % experts, e).start()
        return carry

    load_master.wait()
    stage0(0)
    lax.fori_loop(1, experts, send_code, 0)
    load_hidden.wait()
    HT[...] = hid[...].T

    def tick(i, carry):
        at_stage(i, 4 * HOP, stage_c)
        at_stage(i, 5 * HOP, stage_r1)
        at_stage(i, 6 * HOP, stage_r2)
        at_stage(i, 7 * HOP, stage_r3)
        at_stage(i, 8 * HOP, stage_r4)

        @pl.when(jnp.logical_and(i > 0, i < nc))
        def _():
            stage0(i)

        at_stage(i, HOP, stage1)
        at_stage(i, 2 * HOP, stage2)
        at_stage(i, 3 * HOP, stage3)
        return carry

    lax.fori_loop(0, nc + 8 * HOP, tick, 0)

    def wait_gain(k, carry):
        peer = (e + k) % experts
        g_copy(peer, peer).wait_recv()
        return carry

    lax.fori_loop(1, experts, wait_gain, 0)
    gain = jnp.concatenate([GR[s][0:1, :] for s in range(experts)], axis=0)
    probs_t = PT[...]
    router_out[...] = probs_t * (gain - jnp.sum(probs_t * gain, axis=0, keepdims=True))

    for kind in range(SIB_F + 2):
        left(ss.at[kind], G.at[:, kind])
    left(ss.at[WZ], W.at[:, 0, 0:2])
    left(ss.at[WZF], W.at[:, 0, 0])
    left(ss.at[WY], W.at[:, 0:2])
    left(ss.at[WYF], W.at[:, 0])
    left(ss.at[SF], S.at[:, 0])
    left(ss.at[SR], S.at[:, 0:2])
    for j in range(nc - KEEP, nc):
        release(j)

    def drain_small(k, carry):
        peer = (e + k) % experts
        c_copy(peer, e).wait_send()
        g_copy(peer, e).wait_send()
        return carry

    lax.fori_loop(1, experts, drain_small, 0)


def exchange(out_grad, logits, choices, saved, master):
    t_dev, width = out_grad.shape
    experts = logits.shape[0]
    rows_all, ff = saved.shape
    own = master.shape[0] * 128 // width
    nc = PARTS
    C = width // nc
    vm = pl.BlockSpec(memory_space=pltpu.VMEM)
    hbm = pl.BlockSpec(memory_space=pl.ANY)
    dma = pltpu.SemaphoreType.DMA
    return pl.pallas_call(
        kernel,
        out_shape=(
            jax.ShapeDtypeStruct(master.shape, F32),
            jax.ShapeDtypeStruct((experts, t_dev), F32),
        ),
        in_specs=[hbm, vm, vm, hbm, hbm],
        out_specs=(vm, vm),
        scratch_shapes=[
            pltpu.VMEM((nc, experts, t_dev, C), BF16),
            pltpu.VMEM((nc, NZ, NY, own, C), BF16),
            pltpu.VMEM((KEEP, NZ, NY, own, C), BF16),
            pltpu.VMEM((nc, 2, 2, own, C), BF16),
            pltpu.VMEM((nc, 2, NZ, own, C), BF16),
            pltpu.VMEM((nc, NZ, own, C), BF16),
            pltpu.VMEM((nc, 2, own, C // 2), BF16),
            pltpu.VMEM((nc, 3, own, C), BF16),
            pltpu.VMEM(saved.shape, BF16),
            pltpu.VMEM(master.shape, F32),
            pltpu.VMEM((ff, rows_all), BF16),
            pltpu.VMEM((experts // 2, 4 * (rows_all // experts), 2 * t_dev), BF16),
            pltpu.VMEM((rows_all, C), BF16),
            pltpu.VMEM((rows_all, C), BF16),
            pltpu.VMEM((rows_all, 128), F32),
            pltpu.VMEM((experts, 8, t_dev), F32),
            pltpu.VMEM((experts, 8, t_dev), F32),
            pltpu.VMEM((experts, 8, t_dev), F32),
            pltpu.VMEM((experts, 8, t_dev), F32),
            pltpu.VMEM((experts, t_dev), F32),
            dma((SENDS,)),
            dma((RECVS, nc)),
            dma((KEEP,)),
            dma((nc,)),
            dma((2,)),
            dma((experts,)),
            dma((experts,)),
            dma((experts,)),
            dma((experts,)),
        ],
        compiler_params=pltpu.CompilerParams(
            collective_id=0, has_side_effects=True, vmem_limit_bytes=62 * 1024 * 1024
        ),
    )(out_grad, choices, logits, saved, master)


def shards(out_grad, router_logits, choice_ids, hidden, master, first, second):
    saved = hidden.reshape(hidden.shape[2] * hidden.shape[3], hidden.shape[4])
    shape = master.shape
    master, first, second = lax.optimization_barrier(
        tuple(v.reshape(-1, 128) for v in (master, first, second))
    )
    grad, router_grad = exchange(out_grad, router_logits.T, choice_ids.T, saved, master)
    new_first = beta_one * first + (1.0 - beta_one) * grad
    new_second = beta_two * second + (1.0 - beta_two) * grad * grad
    first_hat = new_first / (1.0 - beta_one**adam_step)
    second_hat = new_second / (1.0 - beta_two**adam_step)
    new_weight = master - learn_rate * (
        first_hat / (jnp.sqrt(second_hat) + epsilon) + decay_rate * master
    )
    return (*(v.reshape(shape) for v in (new_weight, new_first, new_second)), router_grad.T)


def solution(mesh):
    return jax.shard_map(
        shards,
        mesh=mesh,
        in_specs=(
            P(("dp", "expert"), None),
            P(("dp", "expert"), None),
            P(("dp", "expert"), None),
            P("dp", "expert", None, None, None),
            P("dp", "expert", None),
            P("dp", "expert", None),
            P("dp", "expert", None),
        ),
        out_specs=(
            P("dp", "expert", None),
            P("dp", "expert", None),
            P("dp", "expert", None),
            P(("dp", "expert"), None),
        ),
        check_vma=False,
    )
```

```python
import functools

import jax
import jax.numpy as jnp
from jax import lax
from jax.experimental import pallas as pl
from jax.experimental.pallas import tpu as pltpu
from jax.sharding import PartitionSpec as P

beta_one = 0.9
beta_two = 0.95
learn_rate = 0.001
decay_rate = 0.1
epsilon = 1e-08
adam_step = 100.0

MESH = pl.DeviceIdType.MESH
F32 = jnp.float32
BF16 = jnp.bfloat16

NZ, NY, NX = 4, 4, 4
C = 128
AHEAD = 2
LAG_D = (0, 2, 4, 6)
LAG_S = (2, 4, 6)
FIRST = 10
SINGLE = 2
STRAIGHT = 2
T_W, T_CODE, T_H1 = 1, 3, 8
LAG_W = (1, 4)

Z_OWN, XP_OWN, XM_OWN, SIB_OWN = 0, 1, 2, 3
XP_PART, XM_PART, SIB_PART = 4, 5, 6
XP_FWD, XM_FWD = 7, 8
SIB_X = 9
SIB_F = 13
SA, SW, SWZ, SWF, SH, SHF, SF, SR, SY, SC, SG = range(15, 26)
SENDS = 26

(R_A, R_Z, R_X, R_XF, R_SIB, R_WZ, R_WF, R_FZ, R_RZ, R_RY) = range(10)
RECVS = 10
(O_W, O_H, O_HF, O_C, O_G) = range(5)
ONCE = 5


def kernel(
    og_in, ids, logits, hid_in, master_in, grad_out, router_out,
    G, W, WL, PB, FZ, RZ, S, RY, OG, HB, HT, master, OH, ROWS, SCALED, ACC, CS, CR, GP, GQ, GS, GR, PT,
    ss, rs, os_, l2, cs_s, cs_r, gs_s, gs_r,
):
    nc, experts, _, t_dev, _ = G.shape
    rows, ff = HB.shape[1:]
    cap = rows // experts
    d = lax.axis_index("dp")
    e = lax.axis_index("expert")
    z, y = d // NY, d % NY
    zl, x, core = e // (2 * NX), (e // 2) % NX, e % 2
    up = lambda v: (v + 1) % 4
    down = lambda v: (v + 3) % 4
    opp = lambda v: (v + 2) % 4
    eid = lambda a, b, c: a * (2 * NX) + b * 2 + c
    did = lambda a, b: a * NY + b

    part = (d, eid(1 - zl, x, core))
    xp = (d, eid(zl, up(x), core))
    xm = (d, eid(zl, down(x), core))
    sib = (d, eid(zl, x, 1 - core))
    zp = (did(up(z), y), e)
    zm = (did(down(z), y), e)
    zo = (did(opp(z), y), e)
    yp = (did(z, up(y)), e)
    ym = (did(z, down(y)), e)
    yo = (did(z, opp(y)), e)
    along_y = ((up(y), yp), (down(y), ym), (opp(y), yo))

    def rc(send, recv, src, dst, dev):
        return pltpu.make_async_remote_copy(
            src_ref=src, dst_ref=dst, send_sem=send, recv_sem=recv, device_id=dev, device_id_type=MESH
        )

    def arrive(recv, j, ref):
        rc(ss.at[0], rs.at[recv, j], ref, ref, sib).wait_recv()

    def arrive_once(recv, ref):
        rc(ss.at[0], os_.at[recv], ref, ref, sib).wait_recv()

    def left(send, ref):
        rc(ss.at[send], rs.at[0, 0], ref, ref, sib).wait_send()

    own, lanes_of = W.shape[3], NY * nc

    def flat(yy, j):
        return pl.ds(yy * nc + j, own, stride=lanes_of)

    def columns(yy, j):
        return pl.ds(pl.multiple_of((yy * nc + j) * C, C), C)

    load_tokens = pltpu.make_async_copy(og_in, OG, l2.at[0])
    load_master = pltpu.make_async_copy(master_in, master, l2.at[1])
    load_hidden = pltpu.make_async_copy(hid_in, HB.at[y], l2.at[2])
    load_tokens.start()
    load_master.start()
    load_hidden.start()

    barrier = pltpu.get_barrier_semaphore()

    def greet(k, carry):
        pl.semaphore_signal(barrier, inc=1, device_id=(d, (e + k) % experts), device_id_type=MESH)
        return carry

    lax.fori_loop(1, experts, greet, 0)
    for dev in (zp, zm, zo, yp, ym, yo):
        pl.semaphore_signal(barrier, inc=1, device_id=dev, device_id_type=MESH)
    pl.semaphore_wait(barrier, experts - 1 + 6)

    def send_d(kind, recv, j, a, b, dev):
        ref = G.at[j, eid(a, b, core)]
        rc(ss.at[kind], rs.at[recv, j], ref, ref, dev).start()

    def c_copy(peer, source):
        return pltpu.make_async_remote_copy(
            src_ref=CS.at[peer], dst_ref=CR.at[y, source], send_sem=cs_s.at[peer], recv_sem=cs_r.at[source],
            device_id=(d, peer), device_id_type=MESH,
        )

    def g_copy(peer, source):
        return pltpu.make_async_remote_copy(
            src_ref=GS.at[peer], dst_ref=GR.at[source], send_sem=gs_s.at[peer], recv_sem=gs_r.at[source],
            device_id=(d, peer), device_id_type=MESH,
        )

    def share_tokens(j, carry):
        for yy, dev in along_y:
            rc(ss.at[SA], rs.at[R_A, j], OG.at[:, columns(yy, j)], G.at[j, e, y], dev).start()
        G[j, e, y] = OG[:, columns(y, j)]
        return carry

    def tokens0(j):
        arrive(R_A, j, G.at[j, 0, 0:3])
        send_d(Z_OWN, R_Z, j, zl, x, part)
        send_d(XP_OWN, R_X, j, zl, x, xp)
        send_d(XM_OWN, R_X, j, zl, x, xm)
        send_d(SIB_OWN, R_SIB, j, zl, x, sib)

    def tokens1(j):
        arrive(R_Z, j, G.at[j, 0])
        send_d(XP_PART, R_X, j, 1 - zl, x, xp)
        send_d(XM_PART, R_X, j, 1 - zl, x, xm)
        send_d(SIB_PART, R_SIB, j, 1 - zl, x, sib)

    def tokens2(j):
        arrive(R_X, j, G.at[j, 0:4])
        send_d(XP_FWD, R_XF, j, 0, down(x), xp)
        send_d(XM_FWD, R_XF, j, 1, up(x), xm)
        for k, (a, b) in enumerate(((0, down(x)), (1, down(x)), (0, up(x)), (1, up(x)))):
            send_d(SIB_X + k, R_SIB, j, a, b, sib)

    def tokens3(j):
        arrive(R_XF, j, G.at[j, 0:2])
        for k in range(2):
            send_d(SIB_F + k, R_SIB, j, k, opp(x), sib)

    def share_weights():
        def cast(j, carry):
            for yy in range(NY):
                WL[yy, j] = master[flat(yy, j), :].astype(BF16)
            return carry

        lax.fori_loop(0, nc, cast, 0)
        for yy, dev in along_y:
            rc(ss.at[SW], os_.at[O_W], WL.at[yy], W.at[z, y], dev).start()
        W[z, y] = WL[y]

    def weights1(j):
        rc(ss.at[SWZ], rs.at[R_WZ, j], W.at[z, :, j], W.at[z, :, j], zp).start()
        rc(ss.at[SWZ], rs.at[R_WZ, j], W.at[z, :, j], W.at[z, :, j], zm).start()

    def weights2(j):
        arrive(R_WZ, j, W.at[0:2, :, j])
        before, after = W.at[down(z), 0:2, j], W.at[up(z), 2:4, j]
        rc(ss.at[SWF], rs.at[R_WF, j], before, before, zp).start()
        rc(ss.at[SWF], rs.at[R_WF, j], after, after, zm).start()

    def share_hidden():
        load_hidden.wait()
        rc(ss.at[SH], os_.at[O_H], HB.at[y], HB.at[y], yp).start()
        rc(ss.at[SH], os_.at[O_H], HB.at[y], HB.at[y], ym).start()

    def hidden1():
        arrive_once(O_H, HB.at[0:2])
        before, after = HB.at[down(y), 0 : rows // 2], HB.at[up(y), rows // 2 : rows]
        rc(ss.at[SHF], os_.at[O_HF], before, before, yp).start()
        rc(ss.at[SHF], os_.at[O_HF], after, after, ym).start()

    def codes1():
        def wait_code(k, carry):
            peer = (e + k) % experts
            c_copy(peer, peer).wait_recv()
            return carry

        lax.fori_loop(1, experts, wait_code, 0)
        CR[y, pl.ds(e, 1)] = CS[pl.ds(e, 1)]
        for _, dev in along_y:
            rc(ss.at[SC], os_.at[O_C], CR.at[y], CR.at[y], dev).start()

    def setup():
        arrive_once(O_C, CR.at[0:3])
        slots = lax.broadcasted_iota(jnp.int32, (cap, t_dev), 0).astype(F32)
        empty = jnp.zeros((cap, t_dev), F32)

        def select(yy, carry):
            for p in range(experts // 2):
                one, weighted = [], []
                for s in range(2):
                    tile = CR[yy, 2 * p + s]
                    hot = jnp.where(slots == tile[0:1, :], 1.0, 0.0)
                    gate = hot * tile[1:2, :]
                    one.append(jnp.concatenate([hot, empty] if s == 0 else [empty, hot], axis=1))
                    weighted.append(jnp.concatenate([gate, empty] if s == 0 else [empty, gate], axis=1))
                OH[yy, p] = jnp.concatenate(one + weighted, axis=0).astype(BF16)
            return carry

        lax.fori_loop(0, NY, select, 0)

    def setup_hidden():
        arrive_once(O_HF, HB.at[0])
        for yy in range(NY):
            HT[:, yy * rows : (yy + 1) * rows] = HB[yy].T

    def matmuls(j, n):
        for k in range(n):
            arrive(R_SIB, j + k, G.at[j + k, 0:8])
        pair = 2 * cap
        width = n * C

        def side(parts):
            return parts[0] if n == 1 else jnp.concatenate(parts, axis=1)

        def select(yy, carry):
            for p in range(experts // 2):
                tokens = side([G[j + k, 2 * p : 2 * p + 2, yy].reshape(2 * t_dev, C) for k in range(n)])
                picked = jnp.dot(OH[yy, p], tokens, preferred_element_type=F32)
                at = pl.ds(pl.multiple_of(yy * rows + p * pair, 16), pair)
                ROWS[at, 0:width] = picked[:pair].astype(BF16)
                SCALED[at, 0:width] = picked[pair:].astype(BF16)
            return carry

        lax.fori_loop(0, NY, select, 0)
        partial = jnp.dot(HT[...], SCALED[:, 0:width], preferred_element_type=F32).astype(BF16)
        for k in range(n):
            PB[j + k] = partial[:, k * C : (k + 1) * C].reshape(NZ, NY, own, C)
            send_sums(j + k)

        for k in range(n):
            arrive(R_WF, j + k, W.at[0, :, j + k])
        weights = side([W[:, :, j + k].reshape(ff, C) for k in range(n)])

        def through(yy, carry):
            at = pl.ds(pl.multiple_of(yy * rows, rows), rows)
            product = jnp.dot(HB[yy], weights, preferred_element_type=F32) * ROWS[at, 0:width].astype(F32)
            total = product[:, 0:C]
            for k in range(1, n):
                total = total + product[:, k * C : (k + 1) * C]
            ACC[at, :] += total
            return carry

        lax.fori_loop(0, NY, through, 0)

    def send_sums(j):
        @pl.when(j < nc - STRAIGHT)
        def _():
            rc(ss.at[SF], rs.at[R_FZ, j], PB.at[j, opp(z), 2:4], FZ.at[j, 0], zp).start()
            rc(ss.at[SF], rs.at[R_FZ, j], PB.at[j, opp(z), 0:2], FZ.at[j, 1], zm).start()

        @pl.when(j >= nc - STRAIGHT)
        def _():
            rc(ss.at[SF], rs.at[R_RZ, j], PB.at[j, opp(z)], RZ.at[j, 2], zo).start()
            rc(ss.at[SR], rs.at[R_RZ, j], PB.at[j, up(z)], RZ.at[j, 0], zp).start()
            rc(ss.at[SR], rs.at[R_RZ, j], PB.at[j, down(z)], RZ.at[j, 1], zm).start()

    def add(a, b):
        return (a.astype(F32) + b.astype(F32)).astype(BF16)

    def sums1(j):
        @pl.when(j < nc - STRAIGHT)
        def _():
            arrive(R_FZ, j, FZ.at[j])
            PB[j, up(z), 2:4] = add(PB[j, up(z), 2:4], FZ[j, 0])
            rc(ss.at[SR], rs.at[R_RZ, j], PB.at[j, up(z)], RZ.at[j, 0], zp).start()
            PB[j, down(z), 0:2] = add(PB[j, down(z), 0:2], FZ[j, 1])
            rc(ss.at[SR], rs.at[R_RZ, j], PB.at[j, down(z)], RZ.at[j, 1], zm).start()

    def sums2(j):
        @pl.when(j < nc - STRAIGHT)
        def _():
            arrive(R_RZ, j, RZ.at[j, 0:2])
            S[j] = PB[j, z].astype(F32) + RZ[j, 0].astype(F32) + RZ[j, 1].astype(F32)

        @pl.when(j >= nc - STRAIGHT)
        def _():
            arrive(R_RZ, j, RZ.at[j])
            S[j] = PB[j, z].astype(F32) + RZ[j, 0].astype(F32) + RZ[j, 1].astype(F32) + RZ[j, 2].astype(F32)

        for yy, dev in along_y:
            rc(ss.at[SY], rs.at[R_RY, j], S.at[j, yy], RY.at[j, y], dev).start()

    def sums3(j):
        arrive(R_RY, j, RY.at[j, 0:3])
        RY[j, y] = S[j, y]
        for yy in range(NY):
            grad_out[flat(yy, j), :] = RY[j, yy]

    def send_scores():
        slots = lax.broadcasted_iota(jnp.int32, (cap, t_dev), 0).astype(F32)

        def one(yy, carry):
            score = jnp.sum(ACC[pl.ds(pl.multiple_of(yy * rows, rows), rows), :], axis=1, keepdims=True)
            for s in range(experts):
                hot = slots == CR[yy, s][0:1, :]
                GP[yy, s : s + 1, :] = jnp.sum(
                    jnp.where(hot, score[s * cap : (s + 1) * cap, :], 0.0), axis=0, keepdims=True
                )
            return carry

        lax.fori_loop(0, NY, one, 0)
        for yy, dev in along_y:
            rc(ss.at[SG], os_.at[O_G], GP.at[yy], GQ.at[y], dev).start()

    def send_gains():
        arrive_once(O_G, GQ.at[0:3])
        GQ[y] = GP[y]
        total = GQ[0] + GQ[1] + GQ[2] + GQ[3]
        for s in range(experts):
            GS[s, 0:1, :] = total[s : s + 1, :]

        def send(k, carry):
            g_copy((e + k) % experts, e).start()
            return carry

        lax.fori_loop(1, experts, send, 0)
        GR[pl.ds(e, 1)] = GS[pl.ds(e, 1)]

    load_tokens.wait()
    lax.fori_loop(0, nc, share_tokens, 0)

    labels = lax.broadcasted_iota(jnp.int32, (experts, t_dev), 0)
    chosen = jnp.zeros((experts, t_dev), F32)
    for k in range(ids.shape[0]):
        chosen = chosen + jnp.where(ids[k : k + 1, :] == labels, 1.0, 0.0)
    row = lax.broadcasted_iota(jnp.int32, (t_dev, t_dev), 0)
    col = lax.broadcasted_iota(jnp.int32, (t_dev, t_dev), 1)
    earlier = jnp.where(row < col, 1.0, 0.0).astype(BF16)
    slot_of = jnp.dot(chosen.astype(BF16), earlier, preferred_element_type=F32)
    code_t = jnp.where(chosen > 0.5, slot_of, -1.0)
    scores = logits[...]
    powers = jnp.exp(scores - jnp.max(scores, axis=0, keepdims=True))
    probs_t = powers / jnp.sum(powers, axis=0, keepdims=True)
    PT[...] = probs_t
    gate_t = probs_t.astype(BF16).astype(F32)
    CS[...] = jnp.zeros_like(CS)
    GS[...] = jnp.zeros_like(GS)
    ACC[...] = jnp.zeros_like(ACC)
    for s in range(experts):
        CS[s, 0:1, :] = code_t[s : s + 1, :]
        CS[s, 1:2, :] = gate_t[s : s + 1, :]

    def send_code(k, carry):
        c_copy((e + k) % experts, e).start()
        return carry

    lax.fori_loop(1, experts, send_code, 0)
    load_master.wait()
    share_weights()
    share_hidden()

    doubles = (nc - SINGLE) // 2
    last = FIRST + doubles + SINGLE - 1

    def after_matmuls(i, lag, fn):
        u = i - FIRST - lag

        @pl.when(jnp.logical_and(u >= 0, u < doubles))
        def _():
            fn(2 * u)
            fn(2 * u + 1)

        @pl.when(jnp.logical_and(u >= doubles, u < doubles + SINGLE))
        def _():
            fn(u + doubles)

    def once(i, tick, fn):
        @pl.when(i == tick)
        def _():
            fn()

    def tick(i, carry):
        def first_tokens(j, carry):
            tokens0(j)
            return carry

        begin, end = jnp.where(i == 0, 0, jnp.minimum(i + AHEAD, nc)), jnp.minimum(i + AHEAD + 1, nc)
        lax.fori_loop(begin, end, first_tokens, 0)

        for lag, stage in zip(LAG_D[1:], (tokens1, tokens2, tokens3)):
            j = i - lag

            @pl.when(jnp.logical_and(j >= 0, j < nc))
            def _():
                stage(j)

        @pl.when(i == T_W)
        def _():
            arrive_once(O_W, W.at[0, 0:3])

        for lag, stage in zip(LAG_W, (weights1, weights2)):
            j = i - lag

            @pl.when(jnp.logical_and(j >= 0, j < nc))
            def _():
                stage(j)

        once(i, T_CODE, codes1)
        once(i, T_H1, hidden1)
        once(i, FIRST - 1, setup)
        once(i, FIRST, setup_hidden)
        after_matmuls(i, LAG_S[0], sums1)
        after_matmuls(i, LAG_S[1], sums2)
        u = i - FIRST

        @pl.when(jnp.logical_and(u >= 0, u < doubles))
        def _():
            matmuls(2 * u, 2)

        @pl.when(jnp.logical_and(u >= doubles, u < doubles + SINGLE))
        def _():
            matmuls(u + doubles, 1)

        once(i, last, send_scores)
        once(i, last + 2, send_gains)
        after_matmuls(i, LAG_S[2], sums3)
        return carry

    lax.fori_loop(0, last + LAG_S[2] + 1, tick, 0)

    def wait_gain(k, carry):
        peer = (e + k) % experts
        g_copy(peer, peer).wait_recv()
        return carry

    lax.fori_loop(1, experts, wait_gain, 0)
    gain = jnp.concatenate([GR[s][0:1, :] for s in range(experts)], axis=0)
    probs_t = PT[...]
    router_out[...] = probs_t * (gain - jnp.sum(probs_t * gain, axis=0, keepdims=True))

    left(SA, G.at[:, 0, 0:3])
    for kind in range(SIB_F + 2):
        left(kind, G.at[:, kind])
    left(SW, W.at[0, 0:3])
    left(SWZ, W.at[0:2])
    left(SWF, W.at[0])
    left(SH, HB.at[0:2])
    left(SHF, HB.at[0])
    left(SF, PB.at[:, 0])
    left(SR, PB.at[:, 0:2])
    left(SY, S.at[:, 0:3])
    left(SC, CR.at[0:3])
    left(SG, GP.at[0:3])

    def drain_small(k, carry):
        peer = (e + k) % experts
        c_copy(peer, e).wait_send()
        g_copy(peer, e).wait_send()
        return carry

    lax.fori_loop(1, experts, drain_small, 0)


def exchange(out_grad, logits, choices, saved, master):
    t_dev, width = out_grad.shape
    experts = logits.shape[0]
    rows, ff = saved.shape
    own = master.shape[0] * 128 // width
    nc = width // (NY * C)
    cap = rows // experts
    vm = pl.BlockSpec(memory_space=pltpu.VMEM)
    hbm = pl.BlockSpec(memory_space=pl.ANY)
    dma = pltpu.SemaphoreType.DMA
    return pl.pallas_call(
        kernel,
        out_shape=(
            jax.ShapeDtypeStruct(master.shape, F32),
            jax.ShapeDtypeStruct((experts, t_dev), F32),
        ),
        in_specs=[hbm, vm, vm, hbm, hbm],
        out_specs=(vm, vm),
        scratch_shapes=[
            pltpu.VMEM((nc, experts, NY, t_dev, C), BF16),
            pltpu.VMEM((NZ, NY, nc, own, C), BF16),
            pltpu.VMEM((NY, nc, own, C), BF16),
            pltpu.VMEM((nc, NZ, NY, own, C), BF16),
            pltpu.VMEM((nc, 2, 2, own, C), BF16),
            pltpu.VMEM((nc, 3, NY, own, C), BF16),
            pltpu.VMEM((nc, NY, own, C), F32),
            pltpu.VMEM((nc, NY, own, C), F32),
            pltpu.VMEM((t_dev, width), BF16),
            pltpu.VMEM((NY, rows, ff), BF16),
            pltpu.VMEM((ff, NY * rows), BF16),
            pltpu.VMEM(master.shape, F32),
            pltpu.VMEM((NY, experts // 2, 4 * cap, 2 * t_dev), BF16),
            pltpu.VMEM((NY * rows, 2 * C), BF16),
            pltpu.VMEM((NY * rows, 2 * C), BF16),
            pltpu.VMEM((NY * rows, C), F32),
            pltpu.VMEM((experts, 8, t_dev), F32),
            pltpu.VMEM((NY, experts, 8, t_dev), F32),
            pltpu.VMEM((NY, experts, t_dev), F32),
            pltpu.VMEM((NY, experts, t_dev), F32),
            pltpu.VMEM((experts, 8, t_dev), F32),
            pltpu.VMEM((experts, 8, t_dev), F32),
            pltpu.VMEM((experts, t_dev), F32),
            dma((SENDS,)),
            dma((RECVS, nc)),
            dma((ONCE,)),
            dma((3,)),
            dma((experts,)),
            dma((experts,)),
            dma((experts,)),
            dma((experts,)),
        ],
        compiler_params=pltpu.CompilerParams(
            collective_id=0, has_side_effects=True, vmem_limit_bytes=62 * 1024 * 1024
        ),
    )(out_grad, choices, logits, saved, master)


def shards(out_grad, router_logits, choice_ids, hidden, master, first, second):
    saved = hidden.reshape(hidden.shape[2] * hidden.shape[3], hidden.shape[4])
    shape = master.shape
    master, first, second = lax.optimization_barrier(
        tuple(v.reshape(-1, 128) for v in (master, first, second))
    )
    grad, router_grad = exchange(out_grad, router_logits.T, choice_ids.T, saved, master)
    new_first = beta_one * first + (1.0 - beta_one) * grad
    new_second = beta_two * second + (1.0 - beta_two) * grad * grad
    first_hat = new_first / (1.0 - beta_one**adam_step)
    second_hat = new_second / (1.0 - beta_two**adam_step)
    new_weight = master - learn_rate * (
        first_hat / (jnp.sqrt(second_hat) + epsilon) + decay_rate * master
    )
    return (*(v.reshape(shape) for v in (new_weight, new_first, new_second)), router_grad.T)


def solution(mesh):
    return jax.shard_map(
        shards,
        mesh=mesh,
        in_specs=(
            P(("dp", "expert"), None),
            P(("dp", "expert"), None),
            P(("dp", "expert"), None),
            P("dp", "expert", None, None, None),
            P("dp", "expert", None),
            P("dp", "expert", None),
            P("dp", "expert", None),
        ),
        out_specs=(
            P("dp", "expert", None),
            P("dp", "expert", None),
            P("dp", "expert", None),
            P(("dp", "expert"), None),
        ),
        check_vma=False,
    )
```

```python
import functools

import jax
import jax.numpy as jnp
from jax import lax
from jax.experimental import pallas as pl
from jax.experimental.pallas import tpu as pltpu
from jax.sharding import PartitionSpec as P

beta_one = 0.9
beta_two = 0.95
learn_rate = 0.001
decay_rate = 0.1
epsilon = 1e-08
adam_step = 100.0

MESH = pl.DeviceIdType.MESH
F32 = jnp.float32
BF16 = jnp.bfloat16

NZ, NY, NX = 4, 4, 4
C = 128
AHEAD = 3
LAG_D = (0, 1, 3, 5)
LAG_S = (2, 4, 6)
FIRST = 9
SINGLE = 2
STRAIGHT = 2
T_W, T_CODE, T_H1 = 1, 3, 7
LAG_W = (1, 3)

Z_OWN, XP_OWN, XM_OWN, SIB_OWN = 0, 1, 2, 3
XP_PART, XM_PART, SIB_PART = 4, 5, 6
XP_FWD, XM_FWD = 7, 8
SIB_X = 9
SIB_F = 13
SA, SW, SWZ, SWF, SH, SHF, SF, SR, SY, SC, SG = range(15, 26)
SENDS = 26

(R_A, R_Z, R_X, R_XF, R_SIB, R_WZ, R_WF, R_FZ, R_RZ, R_RY) = range(10)
RECVS = 10
(O_W, O_H, O_HF, O_C, O_G) = range(5)
ONCE = 5


def kernel(
    og_in, ids, logits, hid_in, master_in, grad_out, router_out,
    G, W, WL, PB, FZ, RZ, S, RY, OG, HB, HT, master, OH, ROWS, SCALED, ACC, CS, CR, GP, GQ, GS, GR, PT,
    ss, rs, os_, l2, cs_s, cs_r, gs_s, gs_r,
):
    nc, experts, _, t_dev, _ = G.shape
    rows, ff = HB.shape[1:]
    cap = rows // experts
    d = lax.axis_index("dp")
    e = lax.axis_index("expert")
    z, y = d // NY, d % NY
    zl, x, core = e // (2 * NX), (e // 2) % NX, e % 2
    up = lambda v: (v + 1) % 4
    down = lambda v: (v + 3) % 4
    opp = lambda v: (v + 2) % 4
    eid = lambda a, b, c: a * (2 * NX) + b * 2 + c
    did = lambda a, b: a * NY + b

    part = (d, eid(1 - zl, x, core))
    xp = (d, eid(zl, up(x), core))
    xm = (d, eid(zl, down(x), core))
    sib = (d, eid(zl, x, 1 - core))
    zp = (did(up(z), y), e)
    zm = (did(down(z), y), e)
    zo = (did(opp(z), y), e)
    yp = (did(z, up(y)), e)
    ym = (did(z, down(y)), e)
    yo = (did(z, opp(y)), e)
    along_y = ((up(y), yp), (down(y), ym), (opp(y), yo))

    def rc(send, recv, src, dst, dev):
        return pltpu.make_async_remote_copy(
            src_ref=src, dst_ref=dst, send_sem=send, recv_sem=recv, device_id=dev, device_id_type=MESH
        )

    def arrive(recv, j, ref):
        rc(ss.at[0], rs.at[recv, j], ref, ref, sib).wait_recv()

    def arrive_once(recv, ref):
        rc(ss.at[0], os_.at[recv], ref, ref, sib).wait_recv()

    def left(send, ref):
        rc(ss.at[send], rs.at[0, 0], ref, ref, sib).wait_send()

    own, lanes_of = W.shape[3], NY * nc

    def flat(yy, j):
        return pl.ds(yy * nc + j, own, stride=lanes_of)

    def columns(yy, j):
        return pl.ds(pl.multiple_of((yy * nc + j) * C, C), C)

    load_tokens = pltpu.make_async_copy(og_in, OG, l2.at[0])
    load_master = pltpu.make_async_copy(master_in, master, l2.at[1])
    load_hidden = pltpu.make_async_copy(hid_in, HB.at[y], l2.at[2])
    load_tokens.start()
    load_master.start()
    load_hidden.start()

    barrier = pltpu.get_barrier_semaphore()

    def greet(k, carry):
        pl.semaphore_signal(barrier, inc=1, device_id=(d, (e + k) % experts), device_id_type=MESH)
        return carry

    lax.fori_loop(1, experts, greet, 0)
    for dev in (zp, zm, zo, yp, ym, yo):
        pl.semaphore_signal(barrier, inc=1, device_id=dev, device_id_type=MESH)
    pl.semaphore_wait(barrier, experts - 1 + 6)

    def send_d(kind, recv, j, a, b, dev):
        ref = G.at[j, eid(a, b, core)]
        rc(ss.at[kind], rs.at[recv, j], ref, ref, dev).start()

    def c_copy(peer, source):
        return pltpu.make_async_remote_copy(
            src_ref=CS.at[peer], dst_ref=CR.at[y, source], send_sem=cs_s.at[peer], recv_sem=cs_r.at[source],
            device_id=(d, peer), device_id_type=MESH,
        )

    def g_copy(peer, source):
        return pltpu.make_async_remote_copy(
            src_ref=GS.at[peer], dst_ref=GR.at[source], send_sem=gs_s.at[peer], recv_sem=gs_r.at[source],
            device_id=(d, peer), device_id_type=MESH,
        )

    def share_tokens(j, carry):
        for yy, dev in along_y:
            rc(ss.at[SA], rs.at[R_A, j], OG.at[:, columns(yy, j)], G.at[j, e, y], dev).start()
        G[j, e, y] = OG[:, columns(y, j)]
        return carry

    def tokens0(j):
        arrive(R_A, j, G.at[j, 0, 0:3])
        send_d(Z_OWN, R_Z, j, zl, x, part)
        send_d(XP_OWN, R_X, j, zl, x, xp)
        send_d(XM_OWN, R_X, j, zl, x, xm)
        send_d(SIB_OWN, R_SIB, j, zl, x, sib)

    def tokens1(j):
        arrive(R_Z, j, G.at[j, 0])
        send_d(XP_PART, R_X, j, 1 - zl, x, xp)
        send_d(XM_PART, R_X, j, 1 - zl, x, xm)
        send_d(SIB_PART, R_SIB, j, 1 - zl, x, sib)

    def tokens2(j):
        arrive(R_X, j, G.at[j, 0:4])
        send_d(XP_FWD, R_XF, j, 0, down(x), xp)
        send_d(XM_FWD, R_XF, j, 1, up(x), xm)
        for k, (a, b) in enumerate(((0, down(x)), (1, down(x)), (0, up(x)), (1, up(x)))):
            send_d(SIB_X + k, R_SIB, j, a, b, sib)

    def tokens3(j):
        arrive(R_XF, j, G.at[j, 0:2])
        for k in range(2):
            send_d(SIB_F + k, R_SIB, j, k, opp(x), sib)

    def share_weights():
        def cast(j, carry):
            for yy in range(NY):
                WL[yy, j] = master[flat(yy, j), :].astype(BF16)
            return carry

        lax.fori_loop(0, nc, cast, 0)
        for yy, dev in along_y:
            rc(ss.at[SW], os_.at[O_W], WL.at[yy], W.at[z, y], dev).start()
        W[z, y] = WL[y]

    def weights1(j):
        rc(ss.at[SWZ], rs.at[R_WZ, j], W.at[z, :, j], W.at[z, :, j], zp).start()
        rc(ss.at[SWZ], rs.at[R_WZ, j], W.at[z, :, j], W.at[z, :, j], zm).start()

    def weights2(j):
        arrive(R_WZ, j, W.at[0:2, :, j])
        before, after = W.at[down(z), 0:2, j], W.at[up(z), 2:4, j]
        rc(ss.at[SWF], rs.at[R_WF, j], before, before, zp).start()
        rc(ss.at[SWF], rs.at[R_WF, j], after, after, zm).start()

    def share_hidden():
        load_hidden.wait()
        rc(ss.at[SH], os_.at[O_H], HB.at[y], HB.at[y], yp).start()
        rc(ss.at[SH], os_.at[O_H], HB.at[y], HB.at[y], ym).start()

    def hidden1():
        arrive_once(O_H, HB.at[0:2])
        before, after = HB.at[down(y), 0 : rows // 2], HB.at[up(y), rows // 2 : rows]
        rc(ss.at[SHF], os_.at[O_HF], before, before, yp).start()
        rc(ss.at[SHF], os_.at[O_HF], after, after, ym).start()

    def codes1():
        def wait_code(k, carry):
            peer = (e + k) % experts
            c_copy(peer, peer).wait_recv()
            return carry

        lax.fori_loop(1, experts, wait_code, 0)
        CR[y, pl.ds(e, 1)] = CS[pl.ds(e, 1)]
        for _, dev in along_y:
            rc(ss.at[SC], os_.at[O_C], CR.at[y], CR.at[y], dev).start()

    def setup():
        arrive_once(O_C, CR.at[0:3])
        slots = lax.broadcasted_iota(jnp.int32, (cap, t_dev), 0).astype(F32)
        empty = jnp.zeros((cap, t_dev), F32)

        def select(yy, carry):
            for p in range(experts // 2):
                one, weighted = [], []
                for s in range(2):
                    tile = CR[yy, 2 * p + s]
                    hot = jnp.where(slots == tile[0:1, :], 1.0, 0.0)
                    gate = hot * tile[1:2, :]
                    one.append(jnp.concatenate([hot, empty] if s == 0 else [empty, hot], axis=1))
                    weighted.append(jnp.concatenate([gate, empty] if s == 0 else [empty, gate], axis=1))
                OH[yy, p] = jnp.concatenate(one + weighted, axis=0).astype(BF16)
            return carry

        lax.fori_loop(0, NY, select, 0)

    def setup_hidden():
        arrive_once(O_HF, HB.at[0])
        for yy in range(NY):
            HT[:, yy * rows : (yy + 1) * rows] = HB[yy].T

    def matmuls(j, n):
        for k in range(n):
            arrive(R_SIB, j + k, G.at[j + k, 0:8])
        pair = 2 * cap
        width = n * C

        def side(parts):
            return parts[0] if n == 1 else jnp.concatenate(parts, axis=1)

        def select(yy, carry):
            for p in range(experts // 2):
                tokens = side([G[j + k, 2 * p : 2 * p + 2, yy].reshape(2 * t_dev, C) for k in range(n)])
                picked = jnp.dot(OH[yy, p], tokens, preferred_element_type=F32)
                at = pl.ds(pl.multiple_of(yy * rows + p * pair, 16), pair)
                ROWS[at, 0:width] = picked[:pair].astype(BF16)
                SCALED[at, 0:width] = picked[pair:].astype(BF16)
            return carry

        lax.fori_loop(0, NY, select, 0)
        partial = jnp.dot(HT[...], SCALED[:, 0:width], preferred_element_type=F32).astype(BF16)
        for k in range(n):
            PB[j + k] = partial[:, k * C : (k + 1) * C].reshape(NZ, NY, own, C)
            send_sums(j + k)

        for k in range(n):
            arrive(R_WF, j + k, W.at[0, :, j + k])
        weights = side([W[:, :, j + k].reshape(ff, C) for k in range(n)])

        def through(yy, carry):
            at = pl.ds(pl.multiple_of(yy * rows, rows), rows)
            product = jnp.dot(HB[yy], weights, preferred_element_type=F32) * ROWS[at, 0:width].astype(F32)
            total = product[:, 0:C]
            for k in range(1, n):
                total = total + product[:, k * C : (k + 1) * C]
            ACC[at, :] += total
            return carry

        lax.fori_loop(0, NY, through, 0)

    def send_sums(j):
        @pl.when(j < nc - STRAIGHT)
        def _():
            rc(ss.at[SF], rs.at[R_FZ, j], PB.at[j, opp(z), 2:4], FZ.at[j, 0], zp).start()
            rc(ss.at[SF], rs.at[R_FZ, j], PB.at[j, opp(z), 0:2], FZ.at[j, 1], zm).start()

        @pl.when(j >= nc - STRAIGHT)
        def _():
            rc(ss.at[SF], rs.at[R_RZ, j], PB.at[j, opp(z)], RZ.at[j, 2], zo).start()
            rc(ss.at[SR], rs.at[R_RZ, j], PB.at[j, up(z)], RZ.at[j, 0], zp).start()
            rc(ss.at[SR], rs.at[R_RZ, j], PB.at[j, down(z)], RZ.at[j, 1], zm).start()

    def add(a, b):
        return (a.astype(F32) + b.astype(F32)).astype(BF16)

    def sums1(j):
        @pl.when(j < nc - STRAIGHT)
        def _():
            arrive(R_FZ, j, FZ.at[j])
            PB[j, up(z), 2:4] = add(PB[j, up(z), 2:4], FZ[j, 0])
            rc(ss.at[SR], rs.at[R_RZ, j], PB.at[j, up(z)], RZ.at[j, 0], zp).start()
            PB[j, down(z), 0:2] = add(PB[j, down(z), 0:2], FZ[j, 1])
            rc(ss.at[SR], rs.at[R_RZ, j], PB.at[j, down(z)], RZ.at[j, 1], zm).start()

    def sums2(j):
        @pl.when(j < nc - STRAIGHT)
        def _():
            arrive(R_RZ, j, RZ.at[j, 0:2])
            S[j] = PB[j, z].astype(F32) + RZ[j, 0].astype(F32) + RZ[j, 1].astype(F32)

        @pl.when(j >= nc - STRAIGHT)
        def _():
            arrive(R_RZ, j, RZ.at[j])
            S[j] = PB[j, z].astype(F32) + RZ[j, 0].astype(F32) + RZ[j, 1].astype(F32) + RZ[j, 2].astype(F32)

        for yy, dev in along_y:
            rc(ss.at[SY], rs.at[R_RY, j], S.at[j, yy], RY.at[j, y], dev).start()

    def sums3(j):
        arrive(R_RY, j, RY.at[j, 0:3])
        RY[j, y] = S[j, y]
        for yy in range(NY):
            grad_out[flat(yy, j), :] = RY[j, yy]

    def send_scores():
        slots = lax.broadcasted_iota(jnp.int32, (cap, t_dev), 0).astype(F32)

        def one(yy, carry):
            score = jnp.sum(ACC[pl.ds(pl.multiple_of(yy * rows, rows), rows), :], axis=1, keepdims=True)
            for s in range(experts):
                hot = slots == CR[yy, s][0:1, :]
                GP[yy, s : s + 1, :] = jnp.sum(
                    jnp.where(hot, score[s * cap : (s + 1) * cap, :], 0.0), axis=0, keepdims=True
                )
            return carry

        lax.fori_loop(0, NY, one, 0)
        for yy, dev in along_y:
            rc(ss.at[SG], os_.at[O_G], GP.at[yy], GQ.at[y], dev).start()

    def send_gains():
        arrive_once(O_G, GQ.at[0:3])
        GQ[y] = GP[y]
        total = GQ[0] + GQ[1] + GQ[2] + GQ[3]
        for s in range(experts):
            GS[s, 0:1, :] = total[s : s + 1, :]

        def send(k, carry):
            g_copy((e + k) % experts, e).start()
            return carry

        lax.fori_loop(1, experts, send, 0)
        GR[pl.ds(e, 1)] = GS[pl.ds(e, 1)]

    load_tokens.wait()
    lax.fori_loop(0, nc, share_tokens, 0)

    labels = lax.broadcasted_iota(jnp.int32, (experts, t_dev), 0)
    chosen = jnp.zeros((experts, t_dev), F32)
    for k in range(ids.shape[0]):
        chosen = chosen + jnp.where(ids[k : k + 1, :] == labels, 1.0, 0.0)
    row = lax.broadcasted_iota(jnp.int32, (t_dev, t_dev), 0)
    col = lax.broadcasted_iota(jnp.int32, (t_dev, t_dev), 1)
    earlier = jnp.where(row < col, 1.0, 0.0).astype(BF16)
    slot_of = jnp.dot(chosen.astype(BF16), earlier, preferred_element_type=F32)
    code_t = jnp.where(chosen > 0.5, slot_of, -1.0)
    scores = logits[...]
    powers = jnp.exp(scores - jnp.max(scores, axis=0, keepdims=True))
    probs_t = powers / jnp.sum(powers, axis=0, keepdims=True)
    PT[...] = probs_t
    gate_t = probs_t.astype(BF16).astype(F32)
    CS[...] = jnp.zeros_like(CS)
    GS[...] = jnp.zeros_like(GS)
    ACC[...] = jnp.zeros_like(ACC)
    for s in range(experts):
        CS[s, 0:1, :] = code_t[s : s + 1, :]
        CS[s, 1:2, :] = gate_t[s : s + 1, :]

    def send_code(k, carry):
        c_copy((e + k) % experts, e).start()
        return carry

    lax.fori_loop(1, experts, send_code, 0)
    load_master.wait()
    share_weights()
    share_hidden()

    doubles = (nc - SINGLE) // 2
    last = FIRST + doubles + SINGLE - 1

    def after_matmuls(i, lag, fn):
        u = i - FIRST - lag

        @pl.when(jnp.logical_and(u >= 0, u < doubles))
        def _():
            fn(2 * u)
            fn(2 * u + 1)

        @pl.when(jnp.logical_and(u >= doubles, u < doubles + SINGLE))
        def _():
            fn(u + doubles)

    def once(i, tick, fn):
        @pl.when(i == tick)
        def _():
            fn()

    def tick(i, carry):
        def first_tokens(j, carry):
            tokens0(j)
            return carry

        begin, end = jnp.where(i == 0, 0, jnp.minimum(i + AHEAD, nc)), jnp.minimum(i + AHEAD + 1, nc)
        lax.fori_loop(begin, end, first_tokens, 0)

        for lag, stage in zip(LAG_D[1:], (tokens1, tokens2, tokens3)):
            j = i - lag

            @pl.when(jnp.logical_and(j >= 0, j < nc))
            def _():
                stage(j)

        @pl.when(i == T_W)
        def _():
            arrive_once(O_W, W.at[0, 0:3])

        for lag, stage in zip(LAG_W, (weights1, weights2)):
            j = i - lag

            @pl.when(jnp.logical_and(j >= 0, j < nc))
            def _():
                stage(j)

        once(i, T_CODE, codes1)
        once(i, T_H1, hidden1)
        once(i, FIRST - 1, setup)
        once(i, FIRST, setup_hidden)
        after_matmuls(i, LAG_S[0], sums1)
        after_matmuls(i, LAG_S[1], sums2)
        u = i - FIRST

        @pl.when(jnp.logical_and(u >= 0, u < doubles))
        def _():
            matmuls(2 * u, 2)

        @pl.when(jnp.logical_and(u >= doubles, u < doubles + SINGLE))
        def _():
            matmuls(u + doubles, 1)

        once(i, last, send_scores)
        once(i, last + 2, send_gains)
        after_matmuls(i, LAG_S[2], sums3)
        return carry

    lax.fori_loop(0, last + LAG_S[2] + 1, tick, 0)

    def wait_gain(k, carry):
        peer = (e + k) % experts
        g_copy(peer, peer).wait_recv()
        return carry

    lax.fori_loop(1, experts, wait_gain, 0)
    gain = jnp.concatenate([GR[s][0:1, :] for s in range(experts)], axis=0)
    probs_t = PT[...]
    router_out[...] = probs_t * (gain - jnp.sum(probs_t * gain, axis=0, keepdims=True))

    left(SA, G.at[:, 0, 0:3])
    for kind in range(SIB_F + 2):
        left(kind, G.at[:, kind])
    left(SW, W.at[0, 0:3])
    left(SWZ, W.at[0:2])
    left(SWF, W.at[0])
    left(SH, HB.at[0:2])
    left(SHF, HB.at[0])
    left(SF, PB.at[:, 0])
    left(SR, PB.at[:, 0:2])
    left(SY, S.at[:, 0:3])
    left(SC, CR.at[0:3])
    left(SG, GP.at[0:3])

    def drain_small(k, carry):
        peer = (e + k) % experts
        c_copy(peer, e).wait_send()
        g_copy(peer, e).wait_send()
        return carry

    lax.fori_loop(1, experts, drain_small, 0)


def exchange(out_grad, logits, choices, saved, master):
    t_dev, width = out_grad.shape
    experts = logits.shape[0]
    rows, ff = saved.shape
    own = master.shape[0] * 128 // width
    nc = width // (NY * C)
    cap = rows // experts
    vm = pl.BlockSpec(memory_space=pltpu.VMEM)
    hbm = pl.BlockSpec(memory_space=pl.ANY)
    dma = pltpu.SemaphoreType.DMA
    return pl.pallas_call(
        kernel,
        out_shape=(
            jax.ShapeDtypeStruct(master.shape, F32),
            jax.ShapeDtypeStruct((experts, t_dev), F32),
        ),
        in_specs=[hbm, vm, vm, hbm, hbm],
        out_specs=(vm, vm),
        scratch_shapes=[
            pltpu.VMEM((nc, experts, NY, t_dev, C), BF16),
            pltpu.VMEM((NZ, NY, nc, own, C), BF16),
            pltpu.VMEM((NY, nc, own, C), BF16),
            pltpu.VMEM((nc, NZ, NY, own, C), BF16),
            pltpu.VMEM((nc, 2, 2, own, C), BF16),
            pltpu.VMEM((nc, 3, NY, own, C), BF16),
            pltpu.VMEM((nc, NY, own, C), F32),
            pltpu.VMEM((nc, NY, own, C), F32),
            pltpu.VMEM((t_dev, width), BF16),
            pltpu.VMEM((NY, rows, ff), BF16),
            pltpu.VMEM((ff, NY * rows), BF16),
            pltpu.VMEM(master.shape, F32),
            pltpu.VMEM((NY, experts // 2, 4 * cap, 2 * t_dev), BF16),
            pltpu.VMEM((NY * rows, 2 * C), BF16),
            pltpu.VMEM((NY * rows, 2 * C), BF16),
            pltpu.VMEM((NY * rows, C), F32),
            pltpu.VMEM((experts, 8, t_dev), F32),
            pltpu.VMEM((NY, experts, 8, t_dev), F32),
            pltpu.VMEM((NY, experts, t_dev), F32),
            pltpu.VMEM((NY, experts, t_dev), F32),
            pltpu.VMEM((experts, 8, t_dev), F32),
            pltpu.VMEM((experts, 8, t_dev), F32),
            pltpu.VMEM((experts, t_dev), F32),
            dma((SENDS,)),
            dma((RECVS, nc)),
            dma((ONCE,)),
            dma((3,)),
            dma((experts,)),
            dma((experts,)),
            dma((experts,)),
            dma((experts,)),
        ],
        compiler_params=pltpu.CompilerParams(
            collective_id=0, has_side_effects=True, vmem_limit_bytes=62 * 1024 * 1024
        ),
    )(out_grad, choices, logits, saved, master)


def shards(out_grad, router_logits, choice_ids, hidden, master, first, second):
    saved = hidden.reshape(hidden.shape[2] * hidden.shape[3], hidden.shape[4])
    shape = master.shape
    master, first, second = lax.optimization_barrier(
        tuple(v.reshape(-1, 128) for v in (master, first, second))
    )
    grad, router_grad = exchange(out_grad, router_logits.T, choice_ids.T, saved, master)
    new_first = beta_one * first + (1.0 - beta_one) * grad
    new_second = beta_two * second + (1.0 - beta_two) * grad * grad
    first_hat = new_first / (1.0 - beta_one**adam_step)
    second_hat = new_second / (1.0 - beta_two**adam_step)
    new_weight = master - learn_rate * (
        first_hat / (jnp.sqrt(second_hat) + epsilon) + decay_rate * master
    )
    return (*(v.reshape(shape) for v in (new_weight, new_first, new_second)), router_grad.T)


def solution(mesh):
    return jax.shard_map(
        shards,
        mesh=mesh,
        in_specs=(
            P(("dp", "expert"), None),
            P(("dp", "expert"), None),
            P(("dp", "expert"), None),
            P("dp", "expert", None, None, None),
            P("dp", "expert", None),
            P("dp", "expert", None),
            P("dp", "expert", None),
        ),
        out_specs=(
            P("dp", "expert", None),
            P("dp", "expert", None),
            P("dp", "expert", None),
            P(("dp", "expert"), None),
        ),
        check_vma=False,
    )
```

```python
import functools

import jax
import jax.numpy as jnp
from jax import lax
from jax.experimental import pallas as pl
from jax.experimental.pallas import tpu as pltpu
from jax.sharding import PartitionSpec as P

beta_one = 0.9
beta_two = 0.95
learn_rate = 0.001
decay_rate = 0.1
epsilon = 1e-08
adam_step = 100.0

MESH = pl.DeviceIdType.MESH
F32 = jnp.float32
BF16 = jnp.bfloat16

NZ, NY, NX = 4, 4, 4
C = 128
AHEAD = 3
LAG_D = (0, 1, 3, 5)
LAG_S = (2, 4, 6)
FIRST = 9
SINGLE = 2
STRAIGHT = 2
T_W, T_CODE, T_H1 = 1, 3, 6
LAG_W = (1, 3)

Z_OWN, XP_OWN, XM_OWN, SIB_OWN = 0, 1, 2, 3
XP_PART, XM_PART, SIB_PART = 4, 5, 6
XP_FWD, XM_FWD = 7, 8
SIB_X = 9
SIB_F = 13
SA, SW, SWZ, SWF, SH, SHF, SF, SR, SY, SC, SG = range(15, 26)
SENDS = 26

(R_A, R_Z, R_X, R_XF, R_SIB, R_WZ, R_WF, R_FZ, R_RZ, R_RY) = range(10)
RECVS = 10
(O_W, O_H, O_HS, O_HF, O_C, O_G) = range(6)
ONCE = 6


def kernel(
    og_in, ids, logits, hid_in, master_in, grad_out, router_out,
    G, W, WL, PB, FZ, RZ, S, RY, OG, HB, HT, master, OH, ROWS, SCALED, ACC, CS, CR, GP, GQ, GS, GR, PT,
    ss, rs, os_, l2, cs_s, cs_r, gs_s, gs_r,
):
    nc, experts, _, t_dev, _ = G.shape
    rows, ff = HB.shape[1:]
    cap = rows // experts
    d = lax.axis_index("dp")
    e = lax.axis_index("expert")
    z, y = d // NY, d % NY
    zl, x, core = e // (2 * NX), (e // 2) % NX, e % 2
    up = lambda v: (v + 1) % 4
    down = lambda v: (v + 3) % 4
    opp = lambda v: (v + 2) % 4
    eid = lambda a, b, c: a * (2 * NX) + b * 2 + c
    did = lambda a, b: a * NY + b

    part = (d, eid(1 - zl, x, core))
    xp = (d, eid(zl, up(x), core))
    xm = (d, eid(zl, down(x), core))
    sib = (d, eid(zl, x, 1 - core))
    zp = (did(up(z), y), e)
    zm = (did(down(z), y), e)
    zo = (did(opp(z), y), e)
    yp = (did(z, up(y)), e)
    ym = (did(z, down(y)), e)
    yo = (did(z, opp(y)), e)
    along_y = ((up(y), yp), (down(y), ym), (opp(y), yo))

    def rc(send, recv, src, dst, dev):
        return pltpu.make_async_remote_copy(
            src_ref=src, dst_ref=dst, send_sem=send, recv_sem=recv, device_id=dev, device_id_type=MESH
        )

    def arrive(recv, j, ref):
        rc(ss.at[0], rs.at[recv, j], ref, ref, sib).wait_recv()

    def arrive_once(recv, ref):
        rc(ss.at[0], os_.at[recv], ref, ref, sib).wait_recv()

    def left(send, ref):
        rc(ss.at[send], rs.at[0, 0], ref, ref, sib).wait_send()

    own, lanes_of = W.shape[3], NY * nc

    def flat(yy, j):
        return pl.ds(yy * nc + j, own, stride=lanes_of)

    def columns(yy, j):
        return pl.ds(pl.multiple_of((yy * nc + j) * C, C), C)

    load_tokens = pltpu.make_async_copy(og_in, OG, l2.at[0])
    load_master = pltpu.make_async_copy(master_in, master, l2.at[1])
    load_hidden = pltpu.make_async_copy(hid_in, HB.at[y], l2.at[2])
    load_tokens.start()
    load_master.start()
    load_hidden.start()

    barrier = pltpu.get_barrier_semaphore()

    def greet(k, carry):
        pl.semaphore_signal(barrier, inc=1, device_id=(d, (e + k) % experts), device_id_type=MESH)
        return carry

    lax.fori_loop(1, experts, greet, 0)
    for dev in (zp, zm, zo, yp, ym, yo):
        pl.semaphore_signal(barrier, inc=1, device_id=dev, device_id_type=MESH)
    pl.semaphore_wait(barrier, experts - 1 + 6)

    def send_d(kind, recv, j, a, b, dev):
        ref = G.at[j, eid(a, b, core)]
        rc(ss.at[kind], rs.at[recv, j], ref, ref, dev).start()

    def c_copy(peer, source):
        return pltpu.make_async_remote_copy(
            src_ref=CS.at[peer], dst_ref=CR.at[y, source], send_sem=cs_s.at[peer], recv_sem=cs_r.at[source],
            device_id=(d, peer), device_id_type=MESH,
        )

    def g_copy(peer, source):
        return pltpu.make_async_remote_copy(
            src_ref=GS.at[peer], dst_ref=GR.at[source], send_sem=gs_s.at[peer], recv_sem=gs_r.at[source],
            device_id=(d, peer), device_id_type=MESH,
        )

    def share_tokens(j, carry):
        for yy, dev in along_y:
            rc(ss.at[SA], rs.at[R_A, j], OG.at[:, columns(yy, j)], G.at[j, e, y], dev).start()
        G[j, e, y] = OG[:, columns(y, j)]
        return carry

    def tokens0(j):
        arrive(R_A, j, G.at[j, 0, 0:3])
        send_d(Z_OWN, R_Z, j, zl, x, part)
        send_d(XP_OWN, R_X, j, zl, x, xp)
        send_d(XM_OWN, R_X, j, zl, x, xm)
        send_d(SIB_OWN, R_SIB, j, zl, x, sib)

    def tokens1(j):
        arrive(R_Z, j, G.at[j, 0])
        send_d(XP_PART, R_X, j, 1 - zl, x, xp)
        send_d(XM_PART, R_X, j, 1 - zl, x, xm)
        send_d(SIB_PART, R_SIB, j, 1 - zl, x, sib)

    def tokens2(j):
        arrive(R_X, j, G.at[j, 0:4])
        send_d(XP_FWD, R_XF, j, 0, down(x), xp)
        send_d(XM_FWD, R_XF, j, 1, up(x), xm)
        for k, (a, b) in enumerate(((0, down(x)), (1, down(x)), (0, up(x)), (1, up(x)))):
            send_d(SIB_X + k, R_SIB, j, a, b, sib)

    def tokens3(j):
        arrive(R_XF, j, G.at[j, 0:2])
        for k in range(2):
            send_d(SIB_F + k, R_SIB, j, k, opp(x), sib)

    def share_weights():
        def cast(j, carry):
            for yy in range(NY):
                WL[yy, j] = master[flat(yy, j), :].astype(BF16)
            return carry

        lax.fori_loop(0, nc, cast, 0)
        for yy, dev in along_y:
            rc(ss.at[SW], os_.at[O_W], WL.at[yy], W.at[z, y], dev).start()
        W[z, y] = WL[y]

    def weights1(j):
        rc(ss.at[SWZ], rs.at[R_WZ, j], W.at[z, :, j], W.at[z, :, j], zp).start()
        rc(ss.at[SWZ], rs.at[R_WZ, j], W.at[z, :, j], W.at[z, :, j], zm).start()

    def weights2(j):
        arrive(R_WZ, j, W.at[0:2, :, j])
        before, after = W.at[down(z), 0:2, j], W.at[up(z), 2:4, j]
        rc(ss.at[SWF], rs.at[R_WF, j], before, before, zp).start()
        rc(ss.at[SWF], rs.at[R_WF, j], after, after, zm).start()

    def share_hidden():
        load_hidden.wait()
        first, second = HB.at[y, 0 : rows // 2], HB.at[y, rows // 2 : rows]
        rc(ss.at[SH], os_.at[O_H], first, first, yp).start()
        rc(ss.at[SH], os_.at[O_H], second, second, ym).start()
        rc(ss.at[SH], os_.at[O_HS], second, second, yp).start()
        rc(ss.at[SH], os_.at[O_HS], first, first, ym).start()

    def hidden1():
        arrive_once(O_H, HB.at[0])
        before, after = HB.at[down(y), 0 : rows // 2], HB.at[up(y), rows // 2 : rows]
        rc(ss.at[SHF], os_.at[O_HF], before, before, yp).start()
        rc(ss.at[SHF], os_.at[O_HF], after, after, ym).start()

    def codes1():
        def wait_code(k, carry):
            peer = (e + k) % experts
            c_copy(peer, peer).wait_recv()
            return carry

        lax.fori_loop(1, experts, wait_code, 0)
        CR[y, pl.ds(e, 1)] = CS[pl.ds(e, 1)]
        for _, dev in along_y:
            rc(ss.at[SC], os_.at[O_C], CR.at[y], CR.at[y], dev).start()

    def setup():
        arrive_once(O_C, CR.at[0:3])
        slots = lax.broadcasted_iota(jnp.int32, (cap, t_dev), 0).astype(F32)
        empty = jnp.zeros((cap, t_dev), F32)

        def select(yy, carry):
            for p in range(experts // 2):
                one, weighted = [], []
                for s in range(2):
                    tile = CR[yy, 2 * p + s]
                    hot = jnp.where(slots == tile[0:1, :], 1.0, 0.0)
                    gate = hot * tile[1:2, :]
                    one.append(jnp.concatenate([hot, empty] if s == 0 else [empty, hot], axis=1))
                    weighted.append(jnp.concatenate([gate, empty] if s == 0 else [empty, gate], axis=1))
                OH[yy, p] = jnp.concatenate(one + weighted, axis=0).astype(BF16)
            return carry

        lax.fori_loop(0, NY, select, 0)

    def setup_hidden():
        arrive_once(O_HS, HB.at[0])
        arrive_once(O_HF, HB.at[0])
        for yy in range(NY):
            HT[:, yy * rows : (yy + 1) * rows] = HB[yy].T

    def matmuls(j, n):
        for k in range(n):
            arrive(R_SIB, j + k, G.at[j + k, 0:8])
        pair = 2 * cap
        width = n * C

        def side(parts):
            return parts[0] if n == 1 else jnp.concatenate(parts, axis=1)

        def select(yy, carry):
            for p in range(experts // 2):
                tokens = side([G[j + k, 2 * p : 2 * p + 2, yy].reshape(2 * t_dev, C) for k in range(n)])
                picked = jnp.dot(OH[yy, p], tokens, preferred_element_type=F32)
                at = pl.ds(pl.multiple_of(yy * rows + p * pair, 16), pair)
                ROWS[at, 0:width] = picked[:pair].astype(BF16)
                SCALED[at, 0:width] = picked[pair:].astype(BF16)
            return carry

        lax.fori_loop(0, NY, select, 0)
        partial = jnp.dot(HT[...], SCALED[:, 0:width], preferred_element_type=F32).astype(BF16)
        for k in range(n):
            PB[j + k] = partial[:, k * C : (k + 1) * C].reshape(NZ, NY, own, C)
            send_sums(j + k)

        for k in range(n):
            arrive(R_WF, j + k, W.at[0, :, j + k])
        weights = side([W[:, :, j + k].reshape(ff, C) for k in range(n)])

        def through(yy, carry):
            at = pl.ds(pl.multiple_of(yy * rows, rows), rows)
            product = jnp.dot(HB[yy], weights, preferred_element_type=F32) * ROWS[at, 0:width].astype(F32)
            total = product[:, 0:C]
            for k in range(1, n):
                total = total + product[:, k * C : (k + 1) * C]
            ACC[at, :] += total
            return carry

        lax.fori_loop(0, NY, through, 0)

    def send_sums(j):
        @pl.when(j < nc - STRAIGHT)
        def _():
            rc(ss.at[SF], rs.at[R_FZ, j], PB.at[j, opp(z), 2:4], FZ.at[j, 0], zp).start()
            rc(ss.at[SF], rs.at[R_FZ, j], PB.at[j, opp(z), 0:2], FZ.at[j, 1], zm).start()

        @pl.when(j >= nc - STRAIGHT)
        def _():
            rc(ss.at[SF], rs.at[R_RZ, j], PB.at[j, opp(z)], RZ.at[j, 2], zo).start()
            rc(ss.at[SR], rs.at[R_RZ, j], PB.at[j, up(z)], RZ.at[j, 0], zp).start()
            rc(ss.at[SR], rs.at[R_RZ, j], PB.at[j, down(z)], RZ.at[j, 1], zm).start()

    def add(a, b):
        return (a.astype(F32) + b.astype(F32)).astype(BF16)

    def sums1(j):
        @pl.when(j < nc - STRAIGHT)
        def _():
            arrive(R_FZ, j, FZ.at[j])
            PB[j, up(z), 2:4] = add(PB[j, up(z), 2:4], FZ[j, 0])
            rc(ss.at[SR], rs.at[R_RZ, j], PB.at[j, up(z)], RZ.at[j, 0], zp).start()
            PB[j, down(z), 0:2] = add(PB[j, down(z), 0:2], FZ[j, 1])
            rc(ss.at[SR], rs.at[R_RZ, j], PB.at[j, down(z)], RZ.at[j, 1], zm).start()

    def sums2(j):
        @pl.when(j < nc - STRAIGHT)
        def _():
            arrive(R_RZ, j, RZ.at[j, 0:2])
            S[j] = PB[j, z].astype(F32) + RZ[j, 0].astype(F32) + RZ[j, 1].astype(F32)

        @pl.when(j >= nc - STRAIGHT)
        def _():
            arrive(R_RZ, j, RZ.at[j])
            S[j] = PB[j, z].astype(F32) + RZ[j, 0].astype(F32) + RZ[j, 1].astype(F32) + RZ[j, 2].astype(F32)

        for yy, dev in along_y:
            rc(ss.at[SY], rs.at[R_RY, j], S.at[j, yy], RY.at[j, y], dev).start()

    def sums3(j):
        arrive(R_RY, j, RY.at[j, 0:3])
        RY[j, y] = S[j, y]
        for yy in range(NY):
            grad_out[flat(yy, j), :] = RY[j, yy]

    def send_scores():
        slots = lax.broadcasted_iota(jnp.int32, (cap, t_dev), 0).astype(F32)

        def one(yy, carry):
            score = jnp.sum(ACC[pl.ds(pl.multiple_of(yy * rows, rows), rows), :], axis=1, keepdims=True)
            for s in range(experts):
                hot = slots == CR[yy, s][0:1, :]
                GP[yy, s : s + 1, :] = jnp.sum(
                    jnp.where(hot, score[s * cap : (s + 1) * cap, :], 0.0), axis=0, keepdims=True
                )
            return carry

        lax.fori_loop(0, NY, one, 0)
        for yy, dev in along_y:
            rc(ss.at[SG], os_.at[O_G], GP.at[yy], GQ.at[y], dev).start()

    def send_gains():
        arrive_once(O_G, GQ.at[0:3])
        GQ[y] = GP[y]
        total = GQ[0] + GQ[1] + GQ[2] + GQ[3]
        for s in range(experts):
            GS[s, 0:1, :] = total[s : s + 1, :]

        def send(k, carry):
            g_copy((e + k) % experts, e).start()
            return carry

        lax.fori_loop(1, experts, send, 0)
        GR[pl.ds(e, 1)] = GS[pl.ds(e, 1)]

    load_tokens.wait()
    lax.fori_loop(0, nc, share_tokens, 0)

    labels = lax.broadcasted_iota(jnp.int32, (experts, t_dev), 0)
    chosen = jnp.zeros((experts, t_dev), F32)
    for k in range(ids.shape[0]):
        chosen = chosen + jnp.where(ids[k : k + 1, :] == labels, 1.0, 0.0)
    row = lax.broadcasted_iota(jnp.int32, (t_dev, t_dev), 0)
    col = lax.broadcasted_iota(jnp.int32, (t_dev, t_dev), 1)
    earlier = jnp.where(row < col, 1.0, 0.0).astype(BF16)
    slot_of = jnp.dot(chosen.astype(BF16), earlier, preferred_element_type=F32)
    code_t = jnp.where(chosen > 0.5, slot_of, -1.0)
    scores = logits[...]
    powers = jnp.exp(scores - jnp.max(scores, axis=0, keepdims=True))
    probs_t = powers / jnp.sum(powers, axis=0, keepdims=True)
    PT[...] = probs_t
    gate_t = probs_t.astype(BF16).astype(F32)
    CS[...] = jnp.zeros_like(CS)
    GS[...] = jnp.zeros_like(GS)
    ACC[...] = jnp.zeros_like(ACC)
    for s in range(experts):
        CS[s, 0:1, :] = code_t[s : s + 1, :]
        CS[s, 1:2, :] = gate_t[s : s + 1, :]

    def send_code(k, carry):
        c_copy((e + k) % experts, e).start()
        return carry

    lax.fori_loop(1, experts, send_code, 0)
    load_master.wait()
    share_weights()
    share_hidden()

    doubles = (nc - SINGLE) // 2
    last = FIRST + doubles + SINGLE - 1

    def after_matmuls(i, lag, fn):
        u = i - FIRST - lag

        @pl.when(jnp.logical_and(u >= 0, u < doubles))
        def _():
            fn(2 * u)
            fn(2 * u + 1)

        @pl.when(jnp.logical_and(u >= doubles, u < doubles + SINGLE))
        def _():
            fn(u + doubles)

    def once(i, tick, fn):
        @pl.when(i == tick)
        def _():
            fn()

    def tick(i, carry):
        def first_tokens(j, carry):
            tokens0(j)
            return carry

        begin, end = jnp.where(i == 0, 0, jnp.minimum(i + AHEAD, nc)), jnp.minimum(i + AHEAD + 1, nc)
        lax.fori_loop(begin, end, first_tokens, 0)

        for lag, stage in zip(LAG_D[1:], (tokens1, tokens2, tokens3)):
            j = i - lag

            @pl.when(jnp.logical_and(j >= 0, j < nc))
            def _():
                stage(j)

        @pl.when(i == T_W)
        def _():
            arrive_once(O_W, W.at[0, 0:3])

        for lag, stage in zip(LAG_W, (weights1, weights2)):
            j = i - lag

            @pl.when(jnp.logical_and(j >= 0, j < nc))
            def _():
                stage(j)

        once(i, T_CODE, codes1)
        once(i, T_H1, hidden1)
        once(i, FIRST - 1, setup)
        once(i, FIRST, setup_hidden)
        after_matmuls(i, LAG_S[0], sums1)
        after_matmuls(i, LAG_S[1], sums2)
        u = i - FIRST

        @pl.when(jnp.logical_and(u >= 0, u < doubles))
        def _():
            matmuls(2 * u, 2)

        @pl.when(jnp.logical_and(u >= doubles, u < doubles + SINGLE))
        def _():
            matmuls(u + doubles, 1)

        once(i, last, send_scores)
        once(i, last + 2, send_gains)
        after_matmuls(i, LAG_S[2], sums3)
        return carry

    lax.fori_loop(0, last + LAG_S[2] + 1, tick, 0)

    def wait_gain(k, carry):
        peer = (e + k) % experts
        g_copy(peer, peer).wait_recv()
        return carry

    lax.fori_loop(1, experts, wait_gain, 0)
    gain = jnp.concatenate([GR[s][0:1, :] for s in range(experts)], axis=0)
    probs_t = PT[...]
    router_out[...] = probs_t * (gain - jnp.sum(probs_t * gain, axis=0, keepdims=True))

    left(SA, G.at[:, 0, 0:3])
    for kind in range(SIB_F + 2):
        left(kind, G.at[:, kind])
    left(SW, W.at[0, 0:3])
    left(SWZ, W.at[0:2])
    left(SWF, W.at[0])
    left(SH, HB.at[0:2])
    left(SHF, HB.at[0])
    left(SF, PB.at[:, 0])
    left(SR, PB.at[:, 0:2])
    left(SY, S.at[:, 0:3])
    left(SC, CR.at[0:3])
    left(SG, GP.at[0:3])

    def drain_small(k, carry):
        peer = (e + k) % experts
        c_copy(peer, e).wait_send()
        g_copy(peer, e).wait_send()
        return carry

    lax.fori_loop(1, experts, drain_small, 0)


def exchange(out_grad, logits, choices, saved, master):
    t_dev, width = out_grad.shape
    experts = logits.shape[0]
    rows, ff = saved.shape
    own = master.shape[0] * 128 // width
    nc = width // (NY * C)
    cap = rows // experts
    vm = pl.BlockSpec(memory_space=pltpu.VMEM)
    hbm = pl.BlockSpec(memory_space=pl.ANY)
    dma = pltpu.SemaphoreType.DMA
    return pl.pallas_call(
        kernel,
        out_shape=(
            jax.ShapeDtypeStruct(master.shape, F32),
            jax.ShapeDtypeStruct((experts, t_dev), F32),
        ),
        in_specs=[hbm, vm, vm, hbm, hbm],
        out_specs=(vm, vm),
        scratch_shapes=[
            pltpu.VMEM((nc, experts, NY, t_dev, C), BF16),
            pltpu.VMEM((NZ, NY, nc, own, C), BF16),
            pltpu.VMEM((NY, nc, own, C), BF16),
            pltpu.VMEM((nc, NZ, NY, own, C), BF16),
            pltpu.VMEM((nc, 2, 2, own, C), BF16),
            pltpu.VMEM((nc, 3, NY, own, C), BF16),
            pltpu.VMEM((nc, NY, own, C), F32),
            pltpu.VMEM((nc, NY, own, C), F32),
            pltpu.VMEM((t_dev, width), BF16),
            pltpu.VMEM((NY, rows, ff), BF16),
            pltpu.VMEM((ff, NY * rows), BF16),
            pltpu.VMEM(master.shape, F32),
            pltpu.VMEM((NY, experts // 2, 4 * cap, 2 * t_dev), BF16),
            pltpu.VMEM((NY * rows, 2 * C), BF16),
            pltpu.VMEM((NY * rows, 2 * C), BF16),
            pltpu.VMEM((NY * rows, C), F32),
            pltpu.VMEM((experts, 8, t_dev), F32),
            pltpu.VMEM((NY, experts, 8, t_dev), F32),
            pltpu.VMEM((NY, experts, t_dev), F32),
            pltpu.VMEM((NY, experts, t_dev), F32),
            pltpu.VMEM((experts, 8, t_dev), F32),
            pltpu.VMEM((experts, 8, t_dev), F32),
            pltpu.VMEM((experts, t_dev), F32),
            dma((SENDS,)),
            dma((RECVS, nc)),
            dma((ONCE,)),
            dma((3,)),
            dma((experts,)),
            dma((experts,)),
            dma((experts,)),
            dma((experts,)),
        ],
        compiler_params=pltpu.CompilerParams(
            collective_id=0, has_side_effects=True, vmem_limit_bytes=62 * 1024 * 1024
        ),
    )(out_grad, choices, logits, saved, master)


def shards(out_grad, router_logits, choice_ids, hidden, master, first, second):
    saved = hidden.reshape(hidden.shape[2] * hidden.shape[3], hidden.shape[4])
    shape = master.shape
    master, first, second = lax.optimization_barrier(
        tuple(v.reshape(-1, 128) for v in (master, first, second))
    )
    grad, router_grad = exchange(out_grad, router_logits.T, choice_ids.T, saved, master)
    new_first = beta_one * first + (1.0 - beta_one) * grad
    new_second = beta_two * second + (1.0 - beta_two) * grad * grad
    first_hat = new_first / (1.0 - beta_one**adam_step)
    second_hat = new_second / (1.0 - beta_two**adam_step)
    new_weight = master - learn_rate * (
        first_hat / (jnp.sqrt(second_hat) + epsilon) + decay_rate * master
    )
    return (*(v.reshape(shape) for v in (new_weight, new_first, new_second)), router_grad.T)


def solution(mesh):
    return jax.shard_map(
        shards,
        mesh=mesh,
        in_specs=(
            P(("dp", "expert"), None),
            P(("dp", "expert"), None),
            P(("dp", "expert"), None),
            P("dp", "expert", None, None, None),
            P("dp", "expert", None),
            P("dp", "expert", None),
            P("dp", "expert", None),
        ),
        out_specs=(
            P("dp", "expert", None),
            P("dp", "expert", None),
            P("dp", "expert", None),
            P(("dp", "expert"), None),
        ),
        check_vma=False,
    )
```
